32 devices in a mesh: dp: 4 (over y, x), seq: 8 (over z, core).
Axes of the slice: x: 2, y: 2, z: 4, core: 2. Of those that a mesh axis runs over, the one named last changes fastest.
Arguments:
- latents: bfloat16 [8, 2048, 1536], P('dp', 'seq'), may hold values from -6 to 6
- context: bfloat16 [8, 512, 1536], P('dp', 'seq'), may hold values from -6 to 6
- modulation: float32 [8, 6, 1536], P('dp'), may hold values from -4 to 4
- cotangent: bfloat16 [8, 2048, 1536], P('dp', 'seq'), may hold values from -6 to 6
- modtable: bfloat16 [6, 1536], P(None, ('dp', 'seq')), may hold values from -3 to 3
- selfquery: bfloat16 [1536, 1536], P(('dp', 'seq')), may hold values from -0.15625 to 0.15625
- selfkey: bfloat16 [1536, 1536], P(('dp', 'seq')), may hold values from -0.15625 to 0.15625
- selfvalue: bfloat16 [1536, 1536], P(('dp', 'seq')), may hold values from -0.15625 to 0.15625
- selfout: bfloat16 [1536, 1536], P(('dp', 'seq')), may hold values from -1.75 to 1.75
- querygain: bfloat16 [1536], P(('dp', 'seq')), may hold values from 0.099609375 to 1.8984375
- keygain: bfloat16 [1536], P(('dp', 'seq')), may hold values from 0.099609375 to 1.8984375
- normgain: bfloat16 [1536], P(('dp', 'seq')), may hold values from 0.099609375 to 1.8984375
- normbias: bfloat16 [1536], P(('dp', 'seq')), may hold values from -3 to 3
- crossquery: bfloat16 [1536, 1536], P(('dp', 'seq')), may hold values from -0.15625 to 0.15625
- crosskey: bfloat16 [1536, 1536], P(('dp', 'seq')), may hold values from -0.15625 to 0.15625
- crossvalue: bfloat16 [1536, 1536], P(('dp', 'seq')), may hold values from -0.15625 to 0.15625
- crossout: bfloat16 [1536, 1536], P(('dp', 'seq')), may hold values from -0.875 to 0.875
- crossqgain: bfloat16 [1536], P(('dp', 'seq')), may hold values from 0.099609375 to 1.8984375
- crosskgain: bfloat16 [1536], P(('dp', 'seq')), may hold values from 0.099609375 to 1.8984375
- upmatrix: bfloat16 [1536, 8960], P(('dp', 'seq')), may hold values from -0.15625 to 0.15625
- downmatrix: bfloat16 [8960, 1536], P(('dp', 'seq')), may hold values from -0.0625 to 0.0625
Outputs:
- layer_output: bfloat16 [8, 2048, 1536], P('dp', 'seq')
- latents_gradient: float32 [8, 2048, 1536], P('dp', 'seq')
- context_gradient: float32 [8, 512, 1536], P('dp', 'seq')
- modulation_gradient: float32 [8, 6, 1536], P('dp')
- modtable_gradient: float32 [6, 1536], P(None, ('dp', 'seq'))
- selfquery_gradient: float32 [1536, 1536], P(('dp', 'seq'))
- selfkey_gradient: float32 [1536, 1536], P(('dp', 'seq'))
- selfvalue_gradient: float32 [1536, 1536], P(('dp', 'seq'))
- selfout_gradient: float32 [1536, 1536], P(('dp', 'seq'))
- querygain_gradient: float32 [1536], P(('dp', 'seq'))
- keygain_gradient: float32 [1536], P(('dp', 'seq'))
- normgain_gradient: float32 [1536], P(('dp', 'seq'))
- normbias_gradient: float32 [1536], P(('dp', 'seq'))
- crossquery_gradient: float32 [1536, 1536], P(('dp', 'seq'))
- crosskey_gradient: float32 [1536, 1536], P(('dp', 'seq'))
- crossvalue_gradient: float32 [1536, 1536], P(('dp', 'seq'))
- crossout_gradient: float32 [1536, 1536], P(('dp', 'seq'))
- crossqgain_gradient: float32 [1536], P(('dp', 'seq'))
- crosskgain_gradient: float32 [1536], P(('dp', 'seq'))
- upmatrix_gradient: float32 [1536, 8960], P(('dp', 'seq'))
- downmatrix_gradient: float32 [8960, 1536], P(('dp', 'seq'))
The draws below stay inside these ranges and needn't reach their ends.
All inputs are finite; a program needn't handle non-finite values.
Results may differ from the reference program's by a relative error of at most 0.019.
Values may be sent and summed in bfloat16 or wider, within the bound.
No kernel may reach another device: no remote copies, remote signals or barrier semaphores. Data moves between devices by JAX's collectives and lax.ppermute only.
A program may use at most 304 MiB of HBM per device.

```python
import jax
import jax.numpy as jnp
from jax import lax

D = 1536
HEADS = 12
HEAD_DIM = 128
FF = 8960
TEXT = 512
GRID_H = 32
GRID_W = 32
LENGTH = 2048
CLIPS = 8


def steps_of(rng, shape, pieces, low, high):
    loudness = 1.0
    for position, shards_of in pieces:
        steps = jax.random.uniform(jax.random.fold_in(jax.random.fold_in(rng, 6), position), (shards_of,), jnp.float32, low / len(pieces), high / len(pieces))
        loudness = loudness * jnp.repeat(jnp.exp(steps), shape[position] // shards_of).reshape((-1,) + (1,) * (len(shape) - 1 - position))
    return loudness


def noise(own_key, extent, spread, bound, split=(), kind=jnp.bfloat16):
    drawn = spread * jax.random.normal(own_key, extent, jnp.float32)
    if split:
        drawn = drawn * steps_of(own_key, extent, split, -0.22, 0.18)
    return jnp.clip(drawn, -bound, bound).astype(kind)


def setup_inputs(seed: int = 0) -> dict:
    splits = jax.random.split(jax.random.key(seed), 22)
    latents = noise(splits[0], (CLIPS, LENGTH, D), 1.0, 6.0, ((0, 4), (1, 8)))
    context = noise(splits[1], (CLIPS, TEXT, D), 1.0, 6.0, ((0, 4), (1, 8)))
    modulation = noise(splits[2], (CLIPS, 6, D), 0.7, 4.0, ((0, 4),), jnp.float32)
    cotangent = noise(splits[3], (CLIPS, LENGTH, D), 1.0, 6.0, ((0, 4), (1, 8)))
    modtable = noise(splits[4], (6, D), 0.5, 3.0, ((1, 32),))
    selfquery = noise(splits[5], (D, D), D ** -0.5, 0.15625, ((0, 32),))
    selfkey = noise(splits[6], (D, D), D ** -0.5, 0.15625, ((0, 32),))
    selfvalue = noise(splits[7], (D, D), D ** -0.5, 0.15625, ((0, 32),))
    selfout = noise(splits[8], (D, D), (D * 16 // LENGTH) ** -0.5, 1.75, ((0, 32),))
    querygain = jnp.clip(1.0 + 0.18 * jax.random.normal(splits[9], (D,), jnp.float32), 0.099609375, 1.8984375).astype(jnp.bfloat16)
    keygain = jnp.clip(1.0 + 0.18 * jax.random.normal(splits[10], (D,), jnp.float32), 0.099609375, 1.8984375).astype(jnp.bfloat16)
    normgain = jnp.clip(1.0 + 0.18 * jax.random.normal(splits[11], (D,), jnp.float32), 0.099609375, 1.8984375).astype(jnp.bfloat16)
    normbias = noise(splits[12], (D,), 0.5, 3.0, ((0, 32),))
    crossquery = noise(splits[13], (D, D), D ** -0.5, 0.15625, ((0, 32),))
    crosskey = noise(splits[14], (D, D), D ** -0.5, 0.15625, ((0, 32),))
    crossvalue = noise(splits[15], (D, D), D ** -0.5, 0.15625, ((0, 32),))
    crossout = noise(splits[16], (D, D), (D * 16 // TEXT) ** -0.5, 0.875, ((0, 32),))
    crossqgain = jnp.clip(1.0 + 0.18 * jax.random.normal(splits[17], (D,), jnp.float32), 0.099609375, 1.8984375).astype(jnp.bfloat16)
    crosskgain = jnp.clip(1.0 + 0.18 * jax.random.normal(splits[18], (D,), jnp.float32), 0.099609375, 1.8984375).astype(jnp.bfloat16)
    upmatrix = noise(splits[19], (D, FF), D ** -0.5, 0.15625, ((0, 32),))
    downmatrix = noise(splits[20], (FF, D), FF ** -0.5, 0.0625, ((0, 32),))
    return dict(latents=latents, context=context, modulation=modulation, cotangent=cotangent, modtable=modtable, selfquery=selfquery, selfkey=selfkey, selfvalue=selfvalue, selfout=selfout, querygain=querygain, keygain=keygain, normgain=normgain, normbias=normbias, crossquery=crossquery, crosskey=crosskey, crossvalue=crossvalue, crossout=crossout, crossqgain=crossqgain, crosskgain=crosskgain, upmatrix=upmatrix, downmatrix=downmatrix)


@jax.custom_vjp
def low(v):
    return lax.optimization_barrier(v.astype(jnp.bfloat16)).astype(jnp.float32)

@jax.custom_vjp
def low_back(v):
    return v

def low_keep(v):
    return (low(v), None)

def low_pass(kept, grad):
    return (grad,)

def back_keep(v):
    return (v, None)

def back_low(kept, grad):
    return (low(grad),)
low.defvjp(low_keep, low_pass)
low_back.defvjp(back_keep, back_low)
eps_value = 1e-06
highest = lax.Precision.HIGHEST

def layer_norm(values):
    center = values - lax.optimization_barrier(jnp.mean(values, axis=-1, keepdims=True))
    return center * lax.rsqrt(lax.optimization_barrier(jnp.mean(center * center, axis=-1, keepdims=True)) + eps_value)

def rms_norm(values, norm_gain):
    return values * lax.rsqrt(lax.optimization_barrier(jnp.mean(values * values, axis=-1, keepdims=True)) + eps_value) * norm_gain

def frequencies(number):
    return jnp.power(10000.0, -jnp.arange(number, dtype=jnp.float32) / number)

def rotary_tables(positions):
    pair_count = HEAD_DIM // 2
    side_pairs = pair_count // 3
    lead_pairs = pair_count - 2 * side_pairs
    frame_index = (positions // (GRID_H * GRID_W)).astype(jnp.float32)
    row_index = (positions // GRID_W % GRID_H).astype(jnp.float32)
    column_index = (positions % GRID_W).astype(jnp.float32)
    angles = jnp.concatenate([frame_index[:, None] * frequencies(lead_pairs), row_index[:, None] * frequencies(side_pairs), column_index[:, None] * frequencies(side_pairs)], axis=1)
    return (jnp.cos(angles), jnp.sin(angles))

def rotate(values, cosine, sine_table):
    shaped = values.reshape(values.shape[:-1] + (HEADS, HEAD_DIM // 2, 2))
    even_part = shaped[..., 0]
    odd_part = shaped[..., 1]
    cos_rows = cosine[:, None, :]
    sin_rows = sine_table[:, None, :]
    turned = jnp.stack([even_part * cos_rows - odd_part * sin_rows, even_part * sin_rows + odd_part * cos_rows], axis=-1)
    return turned.reshape(values.shape)

def matmul(operand, weights):
    return jnp.einsum('rd,de->re', operand, weights, precision=highest)

def one_head(operands):
    head_query, head_key, head_value = operands
    scores = low_back(jnp.einsum('qd,kd->qk', head_query, head_key, precision=highest)) * HEAD_DIM ** (-0.5)
    max_score = lax.optimization_barrier(jnp.max(scores, axis=-1, keepdims=True))
    exp_score = jnp.exp(scores - max_score)
    attention = exp_score / lax.optimization_barrier(jnp.sum(exp_score, axis=-1, keepdims=True))
    return low_back(jnp.einsum('qk,kd->qd', low(attention), head_value, precision=highest))

def attend(queries, key_rows, value_rows):
    query_heads = queries.reshape(queries.shape[0], HEADS, HEAD_DIM).transpose(1, 0, 2)
    key_heads = key_rows.reshape(key_rows.shape[0], HEADS, HEAD_DIM).transpose(1, 0, 2)
    value_heads = value_rows.reshape(value_rows.shape[0], HEADS, HEAD_DIM).transpose(1, 0, 2)
    outputs = lax.map(jax.checkpoint(one_head), (query_heads, key_heads, value_heads))
    return outputs.transpose(1, 0, 2).reshape(queries.shape[0], HEADS * HEAD_DIM)

def clip_forward(latent_rows, context_rows, modulation_rows, weights):
    modtable, selfquery, selfkey, selfvalue, selfout, querygain, keygain, normgain, normbias, crossquery, crosskey, crossvalue, crossout, crossqgain, crosskgain, upmatrix, downmatrix = weights
    mod_rows = modulation_rows + modtable
    cosine, sine_table = rotary_tables(jnp.arange(LENGTH, dtype=jnp.int32))
    attn_in = low(layer_norm(latent_rows) * (1.0 + mod_rows[1]) + mod_rows[0])
    query_raw = low_back(matmul(attn_in, selfquery))
    key_raw = low_back(matmul(attn_in, selfkey))
    value_raw = low_back(matmul(attn_in, selfvalue))
    query_rot = low(rotate(rms_norm(query_raw, querygain), cosine, sine_table))
    key_rot = low(rotate(rms_norm(key_raw, keygain), cosine, sine_table))
    attended = low(attend(query_rot, key_rot, low(value_raw)))
    hidden_one = latent_rows + low_back(matmul(attended, selfout)) * mod_rows[2]
    cross_in = low(layer_norm(hidden_one) * normgain + normbias)
    cross_query = low(rms_norm(low_back(matmul(cross_in, crossquery)), crossqgain))
    cross_key = low(rms_norm(low_back(matmul(context_rows, crosskey)), crosskgain))
    cross_value = low(low_back(matmul(context_rows, crossvalue)))
    crossed = low(attend(cross_query, cross_key, cross_value))
    hidden_two = hidden_one + low_back(matmul(crossed, crossout))
    mlp_in = low(layer_norm(hidden_two) * (1.0 + mod_rows[4]) + mod_rows[3])
    up_values = low_back(matmul(mlp_in, upmatrix))
    activation = low(jax.nn.gelu(up_values, approximate=True))
    down_values = low_back(matmul(activation, downmatrix))
    return hidden_two + down_values * mod_rows[5]

def widen(array_in):
    return array_in.astype(jnp.float32)

def reference(latents, context, modulation, cotangent, modtable, selfquery, selfkey, selfvalue, selfout, querygain, keygain, normgain, normbias, crossquery, crosskey, crossvalue, crossout, crossqgain, crosskgain, upmatrix, downmatrix):
    weights = jax.tree.map(widen, (modtable, selfquery, selfkey, selfvalue, selfout, querygain, keygain, normgain, normbias, crossquery, crosskey, crossvalue, crossout, crossqgain, crosskgain, upmatrix, downmatrix))

    def forward(latent_all, context_all, modulation_all, weight_set):

        def one_clip(operands):
            latent_rows, context_rows, modulation_rows = operands
            return clip_forward(latent_rows, context_rows, modulation_rows, weight_set)
        return lax.map(jax.checkpoint(one_clip), (latent_all, context_all, modulation_all))
    result, pullback = jax.vjp(forward, widen(latents), widen(context), modulation, weights)
    latent_grad, context_grad, modulation_grad, weight_grads = pullback(widen(cotangent))
    return (result.astype(jnp.bfloat16), latent_grad, context_grad, modulation_grad, weight_grads[0], weight_grads[1], weight_grads[2], weight_grads[3], weight_grads[4], weight_grads[5], weight_grads[6], weight_grads[7], weight_grads[8], weight_grads[9], weight_grads[10], weight_grads[11], weight_grads[12], weight_grads[13], weight_grads[14], weight_grads[15], weight_grads[16])
```

```python
import functools
import math

import jax
import jax.numpy as jnp
import numpy as np
from jax import lax
from jax.experimental import pallas as pl
from jax.experimental.pallas import tpu as pltpu
from jax.sharding import PartitionSpec as P

HEADS = 12
HEAD_DIM = 128
GRID_H = 32
GRID_W = 32
EPS = 1e-06
BF = jnp.bfloat16
F32 = jnp.float32
SCALE = HEAD_DIM ** (-0.5)
SCALE_LOG2 = SCALE * math.log2(math.e)


def layer_norm(values):
    center = values - jnp.mean(values, axis=-1, keepdims=True)
    return center * lax.rsqrt(jnp.mean(center * center, axis=-1, keepdims=True) + EPS)


def layer_norm_back(values, gradient):
    center = values - jnp.mean(values, axis=-1, keepdims=True)
    inverse = lax.rsqrt(jnp.mean(center * center, axis=-1, keepdims=True) + EPS)
    normed = center * inverse
    return inverse * (
        gradient
        - jnp.mean(gradient, axis=-1, keepdims=True)
        - normed * jnp.mean(gradient * normed, axis=-1, keepdims=True)
    )


def gelu_tanh(values):
    return jax.nn.gelu(values, approximate=True)


def dot_nn(left, right, out=F32):
    return lax.dot_general(left, right, (((1,), (0,)), ((), ())), preferred_element_type=F32).astype(out)


def dot_nt(left, right, out=F32):
    return lax.dot_general(left, right, (((1,), (1,)), ((), ())), preferred_element_type=F32).astype(out)


def dot_tn(left, right, out=F32):
    return lax.dot_general(left, right, (((0,), (0,)), ((), ())), preferred_element_type=F32).astype(out)


def rotary_tables(positions):
    pairs = HEAD_DIM // 2
    side = pairs // 3
    lead = pairs - 2 * side

    def rates(number):
        return np.power(np.float32(10000.0), -np.arange(number, dtype=np.float32) / np.float32(number))

    def lanes(start, values):
        row = np.zeros((pairs,), np.float32)
        row[start : start + len(values)] = values
        return np.repeat(row, 2)[None]

    frame = (positions // (GRID_H * GRID_W)).astype(F32)[:, None]
    line = (positions // GRID_W % GRID_H).astype(F32)[:, None]
    column = (positions % GRID_W).astype(F32)[:, None]
    angles = (
        frame * lanes(0, rates(lead))
        + line * lanes(lead, rates(side))
        + column * lanes(lead + side, rates(side))
    )
    even = (np.arange(HEAD_DIM) % 2 == 0)[None]
    sine = jnp.sin(angles)
    return jnp.cos(angles), jnp.where(even, -sine, 0.0), jnp.where(even, 0.0, sine)


def turn(values, cosine, following, previous):
    return (
        values * cosine
        + pltpu.roll(values, HEAD_DIM - 1, 1) * following
        + pltpu.roll(values, 1, 1) * previous
    )


def head_lanes(head):
    return slice(head * HEAD_DIM, (head + 1) * HEAD_DIM)


def row_block(rows):
    return 128 if rows % 128 == 0 else rows


def row_spec(block, width):
    return pl.BlockSpec((block, width), lambda step: (step, 0))


def fixed_spec(width):
    return pl.BlockSpec((1, width), lambda step: (0, 0))


def params(mebibytes):
    return pltpu.CompilerParams(vmem_limit_bytes=mebibytes * 2**20)


def normed_turned(raw_ref, gain_ref, tables, write):
    raw = raw_ref[...]
    inverse = lax.rsqrt(jnp.mean(raw * raw, axis=-1, keepdims=True) + EPS)
    normed = raw * inverse * gain_ref[...]
    for head in range(HEADS):
        piece = normed[:, head_lanes(head)]
        if tables is not None:
            piece = turn(piece, *tables)
        write(head, piece.astype(BF))


def self_post(raw, gain_query, gain_key, tables, groups):
    rows, width = raw.shape[0], raw.shape[1] // 3
    block = row_block(rows)
    per_group = HEADS // groups

    def kernel(query_ref, key_ref, value_ref, gq_ref, gk_ref, cos_ref, next_ref, last_ref, query_out, *outs):
        turns = (cos_ref[...], next_ref[...], last_ref[...])

        def write_query(head, piece):
            query_out[:, head_lanes(head)] = piece

        def write_key(head, piece):
            start = (head % per_group) * 2 * HEAD_DIM
            outs[head // per_group][:, start : start + HEAD_DIM] = piece

        normed_turned(query_ref, gq_ref, turns, write_query)
        normed_turned(key_ref, gk_ref, turns, write_key)
        for head in range(HEADS):
            start = (head % per_group) * 2 * HEAD_DIM + HEAD_DIM
            outs[head // per_group][:, start : start + HEAD_DIM] = value_ref[:, head_lanes(head)].astype(BF)

    out_width = per_group * 2 * HEAD_DIM
    return pl.pallas_call(
        kernel,
        grid=(rows // block,),
        in_specs=[pl.BlockSpec((block, width), lambda step, part=part: (step, part)) for part in range(3)]
        + [fixed_spec(width)] * 2
        + [row_spec(block, HEAD_DIM)] * 3,
        out_specs=[row_spec(block, width)] + [row_spec(block, out_width)] * groups,
        out_shape=[jax.ShapeDtypeStruct((rows, width), BF)]
        + [jax.ShapeDtypeStruct((rows, out_width), BF)] * groups,
        compiler_params=params(32),
        cost_estimate=pl.CostEstimate(flops=rows * width * 20, bytes_accessed=rows * width * 18, transcendentals=0),
        name="self_post",
    )(raw, raw, raw, gain_query, gain_key, *tables)


def query_post(raw, gain):
    rows, width = raw.shape
    block = row_block(rows)

    def kernel(raw_ref, gain_ref, out_ref):
        def write(head, piece):
            out_ref[:, head_lanes(head)] = piece

        normed_turned(raw_ref, gain_ref, None, write)

    return pl.pallas_call(
        kernel,
        grid=(rows // block,),
        in_specs=[row_spec(block, width), fixed_spec(width)],
        out_specs=row_spec(block, width),
        out_shape=jax.ShapeDtypeStruct((rows, width), BF),
        compiler_params=params(24),
        cost_estimate=pl.CostEstimate(flops=rows * width * 10, bytes_accessed=rows * width * 6, transcendentals=0),
        name="query_post",
    )(raw, gain)


def text_post(raw, gain):
    rows, width = raw.shape[0], raw.shape[1] // 2
    block = row_block(rows)

    def kernel(key_ref, value_ref, gain_ref, out_ref):
        def write(head, piece):
            out_ref[:, 2 * head * HEAD_DIM : (2 * head + 1) * HEAD_DIM] = piece

        normed_turned(key_ref, gain_ref, None, write)
        for head in range(HEADS):
            start = (2 * head + 1) * HEAD_DIM
            out_ref[:, start : start + HEAD_DIM] = value_ref[:, head_lanes(head)].astype(BF)

    return pl.pallas_call(
        kernel,
        grid=(rows // block,),
        in_specs=[pl.BlockSpec((block, width), lambda step, part=part: (step, part)) for part in range(2)]
        + [fixed_spec(width)],
        out_specs=row_spec(block, 2 * width),
        out_shape=jax.ShapeDtypeStruct((rows, 2 * width), BF),
        compiler_params=params(24),
        cost_estimate=pl.CostEstimate(flops=rows * width * 10, bytes_accessed=rows * width * 12, transcendentals=0),
        name="text_post",
    )(raw, raw, gain)


def norm_back(raw, gain, gradient):
    inverse = lax.rsqrt(jnp.mean(raw * raw, axis=-1, keepdims=True) + EPS)
    normed = raw * inverse
    gained = gradient * gain
    back = (gained - normed * jnp.mean(gained * normed, axis=-1, keepdims=True)) * inverse
    return back, jnp.sum(gradient * normed, axis=0, keepdims=True)


def turned_back(piece, turns):
    return piece if turns is None else turn(piece, turns[0], -turns[1], -turns[2])


def accumulate(ref, term):
    @pl.when(pl.program_id(0) == 0)
    def _():
        ref[...] = jnp.zeros_like(ref)

    ref[...] += term


def self_query_back(gradients, raw, gain, tables):
    rows, width = raw.shape[0], raw.shape[1] // 3
    block = row_block(rows)
    groups = len(gradients)
    per_group = HEADS // groups

    def kernel(*refs):
        grads = refs[:groups]
        raw_ref, gain_ref, cos_ref, next_ref, last_ref, low_ref, gain_out = refs[groups:]
        turns = (cos_ref[...], next_ref[...], last_ref[...])
        pieces = [
            turned_back(grads[head // per_group][:, head_lanes(head % per_group)], turns)
            for head in range(HEADS)
        ]
        back, term = norm_back(raw_ref[...], gain_ref[...], jnp.concatenate(pieces, axis=1))
        low_ref[...] = back.astype(BF)
        accumulate(gain_out, term)

    return pl.pallas_call(
        kernel,
        grid=(rows // block,),
        in_specs=[row_spec(block, per_group * HEAD_DIM)] * groups
        + [row_spec(block, width), fixed_spec(width)]
        + [row_spec(block, HEAD_DIM)] * 3,
        out_specs=[row_spec(block, width), fixed_spec(width)],
        out_shape=[jax.ShapeDtypeStruct((rows, width), BF), jax.ShapeDtypeStruct((1, width), F32)],
        compiler_params=params(32),
        cost_estimate=pl.CostEstimate(flops=rows * width * 15, bytes_accessed=rows * width * 10, transcendentals=0),
        name="self_query_back",
    )(*gradients, raw, gain, *tables)


def self_keyvalue_back(gradients, raw, gain, tables):
    rows, width = raw.shape[0], raw.shape[1] // 3
    block = row_block(rows)
    groups = len(gradients)
    per_group = HEADS // groups

    def kernel(*refs):
        grads = refs[:groups]
        raw_ref, gain_ref, cos_ref, next_ref, last_ref, low_ref, gain_out = refs[groups:]
        turns = (cos_ref[...], next_ref[...], last_ref[...])
        pieces = []
        for head in range(HEADS):
            start = (head % per_group) * 2 * HEAD_DIM
            ref = grads[head // per_group]
            pieces.append(turned_back(ref[:, start : start + HEAD_DIM], turns))
            value = ref[:, start + HEAD_DIM : start + 2 * HEAD_DIM].astype(BF)
            low_ref[:, width + head * HEAD_DIM : width + (head + 1) * HEAD_DIM] = value
        back, term = norm_back(raw_ref[...], gain_ref[...], jnp.concatenate(pieces, axis=1))
        low_ref[:, :width] = back.astype(BF)
        accumulate(gain_out, term)

    return pl.pallas_call(
        kernel,
        grid=(rows // block,),
        in_specs=[row_spec(block, per_group * 2 * HEAD_DIM)] * groups
        + [pl.BlockSpec((block, width), lambda step: (step, 1)), fixed_spec(width)]
        + [row_spec(block, HEAD_DIM)] * 3,
        out_specs=[row_spec(block, 2 * width), fixed_spec(width)],
        out_shape=[jax.ShapeDtypeStruct((rows, 2 * width), BF), jax.ShapeDtypeStruct((1, width), F32)],
        compiler_params=params(32),
        cost_estimate=pl.CostEstimate(flops=rows * width * 15, bytes_accessed=rows * width * 18, transcendentals=0),
        name="self_keyvalue_back",
    )(*gradients, raw, gain, *tables)


def query_back(gradient, raw, gain):
    rows, width = raw.shape
    block = row_block(rows)

    def kernel(grad_ref, raw_ref, gain_ref, low_ref, gain_out):
        back, term = norm_back(raw_ref[...], gain_ref[...], grad_ref[...])
        low_ref[...] = back.astype(BF)
        accumulate(gain_out, term)

    return pl.pallas_call(
        kernel,
        grid=(rows // block,),
        in_specs=[row_spec(block, width), row_spec(block, width), fixed_spec(width)],
        out_specs=[row_spec(block, width), fixed_spec(width)],
        out_shape=[jax.ShapeDtypeStruct((rows, width), BF), jax.ShapeDtypeStruct((1, width), F32)],
        compiler_params=params(24),
        cost_estimate=pl.CostEstimate(flops=rows * width * 15, bytes_accessed=rows * width * 10, transcendentals=0),
        name="query_back",
    )(gradient, raw, gain)


def text_back(gradient, raw, gain):
    rows, width = raw.shape[0], raw.shape[1] // 2
    block = row_block(rows)

    def kernel(grad_ref, raw_ref, gain_ref, low_ref, gain_out):
        pieces = []
        for head in range(HEADS):
            start = 2 * head * HEAD_DIM
            pieces.append(grad_ref[:, start : start + HEAD_DIM])
            value = grad_ref[:, start + HEAD_DIM : start + 2 * HEAD_DIM].astype(BF)
            low_ref[:, width + head * HEAD_DIM : width + (head + 1) * HEAD_DIM] = value
        back, term = norm_back(raw_ref[...], gain_ref[...], jnp.concatenate(pieces, axis=1))
        low_ref[:, :width] = back.astype(BF)
        accumulate(gain_out, term)

    return pl.pallas_call(
        kernel,
        grid=(rows // block,),
        in_specs=[row_spec(block, 2 * width), row_spec(block, width), fixed_spec(width)],
        out_specs=[row_spec(block, 2 * width), fixed_spec(width)],
        out_shape=[jax.ShapeDtypeStruct((rows, 2 * width), BF), jax.ShapeDtypeStruct((1, width), F32)],
        compiler_params=params(24),
        cost_estimate=pl.CostEstimate(flops=rows * width * 15, bytes_accessed=rows * width * 16, transcendentals=0),
        name="text_back",
    )(gradient, raw, gain)


def attend(query, chunks, base, heads):
    rows = query.shape[0]
    count = len(chunks)
    keys = chunks[0].shape[0]

    def kernel(query_ref, *refs):
        out_ref, log_ref = refs[count:]
        query_head = query_ref[...]
        scores = [dot_nt(ref[:, :HEAD_DIM], query_head) for ref in refs[:count]]
        peak = functools.reduce(
            jnp.maximum, [jnp.max(score, axis=0, keepdims=True) for score in scores]
        )
        shift = peak * SCALE_LOG2
        total = jnp.zeros((1, rows), F32)
        summed = jnp.zeros((HEAD_DIM, rows), F32)
        for ref, score in zip(refs[:count], scores):
            weight = jnp.exp2(score * SCALE_LOG2 - shift)
            total += jnp.sum(weight, axis=0, keepdims=True)
            summed += dot_tn(ref[:, HEAD_DIM:], weight.astype(BF))
        out_ref[...] = (summed / total).T.astype(BF)
        log_ref[0] = shift + jnp.log2(total)

    return pl.pallas_call(
        kernel,
        grid=(heads,),
        in_specs=[pl.BlockSpec((rows, HEAD_DIM), lambda head: (0, base + head))]
        + [pl.BlockSpec((keys, 2 * HEAD_DIM), lambda head: (0, head))] * count,
        out_specs=[
            pl.BlockSpec((rows, HEAD_DIM), lambda head: (0, head)),
            pl.BlockSpec((1, 1, rows), lambda head: (head, 0, 0)),
        ],
        out_shape=[
            jax.ShapeDtypeStruct((rows, heads * HEAD_DIM), BF),
            jax.ShapeDtypeStruct((heads, 1, rows), F32),
        ],
        compiler_params=params(40),
        cost_estimate=pl.CostEstimate(
            flops=heads * rows * keys * count * HEAD_DIM * 4 * 2,
            bytes_accessed=heads * HEAD_DIM * 2 * (2 * rows + 2 * keys * count),
            transcendentals=heads * rows * keys * count,
        ),
        name="attend",
    )(query, *chunks)


def attend_back(query, chunks, gradient, logs, base, heads):
    rows = query.shape[0]
    count = len(chunks)
    keys = chunks[0].shape[0]

    def kernel(query_ref, grad_ref, log_ref, *refs):
        query_grad = refs[count]
        query_head, grad_head = query_ref[...], grad_ref[...]
        shift = log_ref[0]
        weights, value_grads = [], []
        delta = jnp.zeros((1, rows), F32)
        for ref in refs[:count]:
            weight = jnp.exp2(dot_nt(ref[:, :HEAD_DIM], query_head) * SCALE_LOG2 - shift)
            value_grad = dot_nt(ref[:, HEAD_DIM:], grad_head)
            delta += jnp.sum(weight * value_grad, axis=0, keepdims=True)
            weights.append(weight)
            value_grads.append(value_grad)
        summed = jnp.zeros((HEAD_DIM, rows), F32)
        for ref, out, weight, value_grad in zip(refs[:count], refs[count + 1 :], weights, value_grads):
            score_grad = (weight * (value_grad - delta)).astype(BF)
            out[:, :HEAD_DIM] = (dot_nn(score_grad, query_head) * SCALE).astype(BF)
            out[:, HEAD_DIM:] = dot_nn(weight.astype(BF), grad_head).astype(BF)
            summed += dot_tn(ref[:, :HEAD_DIM], score_grad)
        query_grad[...] = (summed * SCALE).T

    return pl.pallas_call(
        kernel,
        grid=(heads,),
        in_specs=[
            pl.BlockSpec((rows, HEAD_DIM), lambda head: (0, base + head)),
            pl.BlockSpec((rows, HEAD_DIM), lambda head: (0, base + head)),
            pl.BlockSpec((1, 1, rows), lambda head: (head, 0, 0)),
        ]
        + [pl.BlockSpec((keys, 2 * HEAD_DIM), lambda head: (0, head))] * count,
        out_specs=[pl.BlockSpec((rows, HEAD_DIM), lambda head: (0, head))]
        + [pl.BlockSpec((keys, 2 * HEAD_DIM), lambda head: (0, head))] * count,
        out_shape=[jax.ShapeDtypeStruct((rows, heads * HEAD_DIM), F32)]
        + [jax.ShapeDtypeStruct((keys, heads * 2 * HEAD_DIM), BF)] * count,
        compiler_params=params(40),
        cost_estimate=pl.CostEstimate(
            flops=heads * rows * keys * count * HEAD_DIM * 10 * 2,
            bytes_accessed=heads * HEAD_DIM * 2 * (5 * rows + 4 * keys * count),
            transcendentals=heads * rows * keys * count,
        ),
        name="attend_back",
    )(query, gradient, logs, *chunks)


def place_rows(numbers, left, right, rows, total):
    slots, _, right_width = right[0][0].shape
    left_width = left[0][0].shape[2]
    count = len(left)

    def kernel(numbers_ref, *refs):
        whole_ref, small_ref = refs[4 * count :]
        step = pl.program_id(0)
        for at in range(count):
            for core in range(2):

                @pl.when((step // slots == at) & (numbers_ref[0] == core))
                def _():
                    for other in range(2):
                        place = pl.ds((other ^ core) * rows, rows)
                        left_ref, right_ref = refs[4 * at + other], refs[4 * at + 2 + other]
                        whole_ref[place, :right_width] = left_ref[0, :, :right_width]
                        whole_ref[place, right_width:] = right_ref[0]
                        small_ref[place] = left_ref[0, :, right_width:]

    def source(at, width):
        return pl.BlockSpec(
            (1, rows, width),
            lambda step, numbers_ref: (jnp.clip(step - at * slots, 0, slots - 1), 0, 0),
        )

    def index(step, numbers_ref):
        return (numbers_ref[step + 1], 0)

    in_specs, arrays = [], []
    for at in range(count):
        in_specs += [source(at, left_width)] * 2 + [source(at, right_width)] * 2
        arrays += [*left[at], *right[at]]
    return pl.pallas_call(
        kernel,
        grid_spec=pltpu.PrefetchScalarGridSpec(
            num_scalar_prefetch=1,
            grid=(count * slots,),
            in_specs=in_specs,
            out_specs=[
                pl.BlockSpec((2 * rows, 2 * right_width), index),
                pl.BlockSpec((2 * rows, left_width - right_width), index),
            ],
        ),
        out_shape=[
            jax.ShapeDtypeStruct((total, 2 * right_width), BF),
            jax.ShapeDtypeStruct((total, left_width - right_width), BF),
        ],
        compiler_params=params(32),
        cost_estimate=pl.CostEstimate(flops=0, bytes_accessed=8 * total * right_width, transcendentals=0),
        name="place_rows",
    )(numbers, *arrays)


def after(value, *others):
    return lax.optimization_barrier((value,) + others)[0]


def together(*values):
    return lax.optimization_barrier(values)


class Plan:
    def __init__(self, mesh):
        self.dp_n = mesh.shape["dp"]
        self.seq_n = mesh.shape["seq"]
        self.total = self.dp_n * self.seq_n
        self.half = self.seq_n // 2
        self.columns = self.seq_n // 2
        self.groups = 3 if self.half <= 4 else 1
        self.dp_bits = [1 << i for i in range(self.dp_n.bit_length() - 1)]
        self.group_bits = [1 << i for i in range(self.half.bit_length() - 1)]

    def start(self):
        self.dp = lax.axis_index("dp")
        self.seq = lax.axis_index("seq")
        self.me = self.dp * self.seq_n + self.seq
        self.core = self.seq % 2
        self.column = self.seq // 2
        self.top = self.seq // self.half

    def over_seq(self, value, offset):
        return lax.ppermute(value, "seq", [(i, i ^ offset) for i in range(self.seq_n)])

    def over_dp(self, value, offset):
        return lax.ppermute(value, "dp", [(i, i ^ offset) for i in range(self.dp_n)])


    def shift(self, value):
        own = lax.dynamic_index_in_dim(value, self.top, 0, keepdims=False)
        other = lax.dynamic_index_in_dim(value, 1 - self.top, 0, keepdims=False)
        return jnp.concatenate([own, self.over_seq(other, self.half)], axis=0)

    def unshift(self, value):
        rows = value.shape[0] // 2
        own, other = value[:rows], self.over_seq(value[rows:], self.half)
        return jnp.where(self.top == 0, jnp.stack([own, other]), jnp.stack([other, own]))


    def group_gather(self, value, *behind):
        held = {0: after(value, *behind) if behind else value}
        for bit in reversed(self.group_bits):
            held.update({at ^ bit: self.over_seq(one, bit) for at, one in list(held.items())})
        return held

    def group_scatter(self, held):
        held = dict(held)
        for bit in self.group_bits:
            for at in sorted(held):
                if at & bit:
                    sent = self.over_seq(held.pop(at).astype(BF), bit)
                    held[at ^ bit] = held[at ^ bit].astype(F32) + sent.astype(F32)
        return held[0]


    def gather_columns(self, shard):
        return jnp.stack([shard] + [self.over_seq(shard, 2 * k) for k in range(1, self.columns)])

    def gather_dp(self, sides, orders):
        sides, offsets = list(sides), [[0] for _ in sides]
        for number in range(len(orders[0])):
            received = together(*[self.over_dp(one, order[number]) for one, order in zip(sides, orders)])
            for i, order in enumerate(orders):
                flipped = [at ^ order[number] for at in offsets[i]]
                if number + 1 < len(order):
                    sides[i], offsets[i] = jnp.concatenate([sides[i], received[i]]), offsets[i] + flipped
                else:
                    sides[i], offsets[i] = [sides[i], received[i]], [offsets[i], flipped]
        return sides, offsets

    def gather_core(self, held):
        return [(one, self.over_seq(one, 1)) for one in held]

    def gather_place(self, left, left_offsets, right, right_offsets):
        slots = self.columns
        rows, width = right[0][0].shape[1:]

        def by_offset(held, offsets):
            return {
                at: tuple(one[i * slots : (i + 1) * slots] for one in pair)
                for pair, ats in zip(held, offsets)
                for i, at in enumerate(ats)
            }

        left, right = by_offset(left, left_offsets), by_offset(right, right_offsets)
        if rows % 16 == 0:
            blocks = [(self.dp ^ at) * slots + (self.column ^ slot) for at in left for slot in range(slots)]
            numbers = jnp.stack([self.core] + blocks).astype(jnp.int32)
            return place_rows(
                numbers, list(left.values()), [right[at] for at in left], rows, self.total * rows
            )
        wholes = []
        for held in (left, right):
            pieces = [
                held[number // self.seq_n][number % 2][(number % self.seq_n) // 2]
                for number in range(self.total)
            ]
            stacked = jnp.stack(pieces)

            def place(number, out):
                return lax.dynamic_update_index_in_dim(
                    out, self.pick(stacked, number, 0), number ^ self.me, 0
                )

            ordered = lax.fori_loop(0, self.total, place, jnp.zeros_like(stacked))
            wholes.append(ordered.reshape(self.total * rows, -1))
        left, right = wholes
        return jnp.concatenate([left[:, :width], right], axis=1), left[:, width:]

    def xor_order(self, pieces, number):
        bit = 1
        while bit < len(pieces):
            swapped = (number // bit) % 2 == 1
            pieces = [jnp.where(swapped, pieces[i ^ bit], pieces[i]) for i in range(len(pieces))]
            bit *= 2
        return pieces

    def pick(self, value, number, axis):
        return lax.dynamic_index_in_dim(value, number, axis, keepdims=False)

    def scatter_columns(self, value, axis, wire):
        total = self.pick(value, self.column, axis).astype(F32)
        for k in range(1, self.columns):
            sent = self.over_seq(self.pick(value, self.column ^ k, axis).astype(wire), 2 * k)
            total = total + sent.astype(F32)
        return total


    def scatter_core(self, value):
        bits = len(self.dp_bits)
        value = value.reshape((2,) * bits + (self.columns, 2, value.shape[0] // self.total, value.shape[1]))
        sent = self.over_seq(self.pick(value, 1 - self.core, bits + 1), 1)
        return self.pick(value, self.core, bits + 1), sent

    def scatter_dp(self, halves, done, bit):
        value = (halves[0].astype(F32) + halves[1].astype(F32)).astype(BF)
        axis = [one for one in reversed(self.dp_bits) if one not in done].index(bit)
        mine = (self.dp // bit) % 2
        sent = self.over_dp(self.pick(value, 1 - mine, axis), bit)
        return self.pick(value, mine, axis), sent

    def scatter_dps(self, halves, bits, done=()):
        for bit in bits:
            halves = self.scatter_dp(halves, done, bit)
            done = done + (bit,)
        return halves

    def scatter_last(self, halves):
        return self.scatter_columns(halves[0].astype(F32) + halves[1].astype(F32), 0, BF)


def body(
    plan,
    latents,
    context,
    modulation,
    cotangent,
    modtable,
    selfquery,
    selfkey,
    selfvalue,
    selfout,
    querygain,
    keygain,
    normgain,
    normbias,
    crossquery,
    crosskey,
    crossvalue,
    crossout,
    crossqgain,
    crosskgain,
    upmatrix,
    downmatrix,
):
    plan.start()
    width = latents.shape[2]
    dp_n, seq_n, columns = plan.dp_n, plan.seq_n, plan.columns
    everywhere = ("dp", "seq")
    rows_one = latents.shape[1]
    shard_rows = selfquery.shape[0]
    hidden = upmatrix.shape[1]
    part = hidden // dp_n
    xy, yx = plan.dp_bits, list(reversed(plan.dp_bits))

    small = jnp.concatenate(
        [modtable.T]
        + [gain[:, None] for gain in (querygain, keygain, normgain, normbias, crossqgain, crosskgain)]
        + [jnp.zeros((shard_rows, HEAD_DIM - 12), BF)],
        axis=1,
    )
    middle = 3 * width // 2
    side = jnp.concatenate([selfquery, selfkey, selfvalue], axis=1)
    both = plan.gather_columns(jnp.concatenate([side[:, :middle], small, side[:, middle:]], axis=1))
    token_rows = plan.shift(latents)
    both, token_rows = together(both, token_rows)
    (left_held, right_held), (left_offsets, right_offsets) = plan.gather_dp(
        (both[:, :, : middle + HEAD_DIM], both[:, :, middle + HEAD_DIM :]), (xy, yx)
    )
    left_held, right_held = plan.gather_core(left_held), plan.gather_core(right_held)
    whole_self, small_all = plan.gather_place(left_held, left_offsets, right_held, right_offsets)
    small_all = small_all.T[:12].astype(F32)

    others = jnp.concatenate([selfout, crossquery, crossout, crosskey, crossvalue], axis=1)
    whole_others = lax.all_gather(others, everywhere, axis=0, tiled=True)
    whole_selfout, whole_crossquery, whole_crossout = [
        whole_others[:, i * width : (i + 1) * width] for i in range(3)
    ]
    whole_crosstext = whole_others[:, 3 * width :]

    up_rows = after(upmatrix, both)
    up_parts = [
        lax.dynamic_slice_in_dim(up_rows, (plan.dp ^ j) * part, part, 1) for j in range(dp_n)
    ]
    up_parts = [plan.over_dp(one, j) if j else one for j, one in enumerate(up_parts)]
    up_shard = jnp.concatenate(plan.xor_order(up_parts, plan.dp), axis=0)
    shifted = plan.shift(after(jnp.concatenate([cotangent, context], axis=1), both))
    down_shard, whole_self, shifted, _ = together(downmatrix, whole_self, shifted, whole_others)
    whole_down = lax.all_gather(down_shard, "seq", axis=0, tiled=True)
    text_one = context.shape[1]
    step = rows_one + text_one
    grad_rows = jnp.concatenate([shifted[:rows_one], shifted[step : step + rows_one]])
    text_rows = jnp.concatenate([shifted[rows_one:step], shifted[step + rows_one :]])

    mod_rows = lax.dynamic_index_in_dim(modulation, plan.top, 0, keepdims=False) + small_all[:6]
    shift_a, scale_a, gate_a, shift_m, scale_m, gate_m = [mod_rows[i : i + 1] for i in range(6)]
    gain_query, gain_key, gain_norm, bias_norm, gain_crossq, gain_crossk = [
        small_all[i : i + 1] for i in range(6, 12)
    ]
    span = jnp.arange(rows_one, dtype=jnp.int32)
    positions = jnp.concatenate(
        [plan.seq * rows_one + span, (plan.seq ^ plan.half) * rows_one + span]
    )
    tables = rotary_tables(positions)

    latent_rows = token_rows.astype(F32)
    normed_a = layer_norm(latent_rows)
    attn_in = (normed_a * (1.0 + scale_a) + shift_a).astype(BF)
    self_raw = dot_nn(attn_in, whole_self)
    queries, *keyvalues = self_post(self_raw, gain_query, gain_key, tables, plan.groups)
    per_group = HEADS // plan.groups
    gathered = []
    for one in keyvalues:
        behind = [gathered[-1][plan.group_bits[-1]]] if gathered else []
        gathered.append(plan.group_gather(one, *behind))
    up_shard = after(up_shard, gathered[0][plan.group_bits[-1]])
    whole_up = lax.all_gather(up_shard, "seq", axis=0, tiled=True)
    whole_up = (
        whole_up.reshape(seq_n, dp_n, shard_rows, part)
        .transpose(1, 0, 2, 3)
        .reshape(plan.total * shard_rows, part)
    )
    out_grad = grad_rows.astype(F32)
    down_grad = (out_grad * gate_m).astype(BF)
    down_grads = [down_grad] + [plan.over_dp(down_grad, j) for j in range(1, dp_n)]
    self_outs, self_logs = [], []
    for group in range(plan.groups):
        out, logs = attend(queries, list(gathered[group].values()), group * per_group, per_group)
        self_outs.append(out)
        self_logs.append(logs)
    *self_outs, down_grads = together(*self_outs, down_grads)
    attended = jnp.concatenate(self_outs, axis=1)
    self_branch = dot_nn(attended, whole_selfout)
    hidden_one = latent_rows + self_branch * gate_a

    text_raw = dot_nn(text_rows, whole_crosstext)
    cross_gathered = plan.group_gather(text_post(text_raw, gain_crossk))
    cross_in = (layer_norm(hidden_one) * gain_norm + bias_norm).astype(BF)
    crossq_raw = dot_nn(cross_in, whole_crossquery)
    cross_queries = query_post(crossq_raw, gain_crossq)
    crossed, cross_logs = attend(cross_queries, list(cross_gathered.values()), 0, HEADS)
    hidden_two = hidden_one + dot_nn(crossed, whole_crossout)

    act_grads = [dot_nt(one, whole_down) for one in down_grads]
    normed_m = layer_norm(hidden_two)
    mlp_in = (normed_m * (1.0 + scale_m) + shift_m).astype(BF)
    mlp_ins = [mlp_in] + [plan.over_dp(mlp_in, j) for j in range(1, dp_n)]
    activations, up_grads, mlp_grads = [], [], []
    for j in range(dp_n):
        up_values = dot_nn(mlp_ins[j], whole_up)
        activation, gelu_back = jax.vjp(gelu_tanh, up_values)
        activations.append(activation.astype(BF))
        up_grads.append(gelu_back(act_grads[j])[0].astype(BF))
        mlp_grads.append(dot_nt(up_grads[j], whole_up, BF if j else F32))
    mlp_sent = [plan.over_dp(mlp_grads[j], j) for j in range(1, dp_n)]

    up_in, down_in, _ = together(jnp.concatenate(mlp_ins), jnp.concatenate(activations), mlp_grads[0])
    up_term = dot_tn(up_in, jnp.concatenate(up_grads), BF)
    down_term = dot_tn(down_in, jnp.concatenate(down_grads), BF)
    *mlp_sent, up_term, down_term = together(*mlp_sent, up_term, down_term)
    mlp_grad = mlp_grads[0] + sum(one.astype(F32) for one in mlp_sent)
    downmatrix_gradient = lax.psum_scatter(down_term, "seq", scatter_dimension=0, tiled=True).astype(F32)
    up_term = (
        up_term.reshape(dp_n, seq_n, shard_rows, part)
        .transpose(1, 0, 2, 3)
        .reshape(plan.total * shard_rows, part)
    )
    up_term = lax.psum_scatter(up_term, "seq", scatter_dimension=0, tiled=True)
    up_term = up_term.reshape(dp_n, shard_rows, part)

    shift_m_grad = jnp.sum(mlp_grad, axis=0)
    scale_m_grad = jnp.sum(mlp_grad * normed_m, axis=0)
    two_grad = out_grad + layer_norm_back(hidden_two, mlp_grad * (1.0 + scale_m))
    cross_grad = two_grad.astype(BF)
    crossed_grad = dot_nt(cross_grad, whole_crossout, BF)
    crossout_sum = plan.scatter_core(dot_tn(crossed, cross_grad, BF))
    crossq_grad, *cross_parts = attend_back(
        cross_queries, list(cross_gathered.values()), crossed_grad, cross_logs, 0, HEADS
    )
    crossq_grad, crossout_sum = together(crossq_grad, crossout_sum)
    crossout_sum = plan.scatter_dp(crossout_sum, (), xy[0])
    cross_own = plan.group_scatter(dict(zip(cross_gathered, cross_parts)))
    crossq_low, crossq_gaingrad = query_back(crossq_grad, crossq_raw, gain_crossq)
    crossq_sum = plan.scatter_core(dot_tn(cross_in, crossq_low, BF))
    crossin_grad = dot_nt(crossq_low, whole_crossquery)
    normgain_grad = jnp.sum(crossin_grad * layer_norm(hidden_one), axis=0)
    normbias_grad = jnp.sum(crossin_grad, axis=0)
    one_grad = two_grad + layer_norm_back(hidden_one, crossin_grad * gain_norm)
    gate_a_grad = jnp.sum(one_grad * self_branch, axis=0)
    branch_grad = (one_grad * gate_a).astype(BF)
    branch_grad, crossq_sum, crossout_sum, cross_own = together(branch_grad, crossq_sum, crossout_sum, cross_own)
    crossq_sum = plan.scatter_dp(crossq_sum, (), yx[0])
    crossout_sum = plan.scatter_dps(crossout_sum, xy[1:], (xy[0],))
    text_low, crossk_gaingrad = text_back(cross_own, text_raw, gain_crossk)
    text_gradients = lax.psum_scatter(
        dot_tn(text_rows, text_low, BF), everywhere, scatter_dimension=0, tiled=True
    ).astype(F32)
    context_gradient = plan.unshift(dot_nt(text_low, whole_crosstext, BF))

    attended_grad = dot_nt(branch_grad, whole_selfout, BF)
    selfout_sum = plan.scatter_core(dot_tn(attended, branch_grad, BF))
    query_grads, keyvalue_grads = [], []
    for group in range(plan.groups):
        query_grad, *parts = attend_back(
            queries,
            list(gathered[group].values()),
            attended_grad,
            self_logs[group],
            group * per_group,
            per_group,
        )
        if group == 0:
            query_grad, crossout_sum, crossq_sum, context_gradient, selfout_sum = together(
                query_grad, crossout_sum, crossq_sum, context_gradient, selfout_sum
            )
            crossout_gradient = plan.scatter_last(crossout_sum)
            crossq_sum = plan.scatter_dps(crossq_sum, yx[1:], (yx[0],))
            selfout_sum = plan.scatter_dp(selfout_sum, (), xy[0])
        query_grads.append(query_grad)
        keyvalue_grads.append(plan.group_scatter(dict(zip(gathered[group], parts))))
    query_low, query_gaingrad = self_query_back(query_grads, self_raw, gain_query, tables)
    query_low, crossout_gradient, crossq_sum, selfout_sum = together(
        query_low, crossout_gradient, crossq_sum, selfout_sum
    )
    crossquery_gradient = plan.scatter_last(crossq_sum)
    selfout_sum = plan.scatter_dps(selfout_sum, xy[1:], (xy[0],))
    query_sum = plan.scatter_core(dot_tn(attn_in, query_low, BF))
    attn_grad = dot_nt(query_low, whole_self[:, :width])

    *activations, query_sum = together(*activations, query_sum)
    query_sum = plan.scatter_dp(query_sum, (), yx[0])
    down_all = [dot_nn(activations[j], whole_down, BF if j else F32) for j in range(dp_n)]
    down_sent = [plan.over_dp(down_all[j], j) for j in range(1, dp_n)]

    keyvalue_low, key_gaingrad = self_keyvalue_back(keyvalue_grads, self_raw, gain_key, tables)
    key_sum = plan.scatter_core(dot_tn(attn_in, keyvalue_low[:, :width], BF))
    value_sum = plan.scatter_core(dot_tn(attn_in, keyvalue_low[:, width:], BF))
    kept_low, _, _ = together(keyvalue_low, key_sum[0], value_sum[0])
    attn_grad = attn_grad + dot_nt(kept_low, whole_self[:, width:])
    key_sum, value_sum, selfout_sum, query_sum = together(key_sum, value_sum, selfout_sum, query_sum)
    key_sum = plan.scatter_dp(key_sum, (), xy[0])
    value_sum = plan.scatter_dp(value_sum, (), yx[0])
    down_values = down_all[0] + sum(one.astype(F32) for one in down_sent)
    layer_low = (hidden_two + down_values * gate_m).astype(BF)
    gate_m_grad = jnp.sum(out_grad * down_values, axis=0)
    selfout_gradient = plan.scatter_last(selfout_sum)
    query_sum = plan.scatter_dps(query_sum, yx[1:], (yx[0],))
    shift_a_grad = jnp.sum(attn_grad, axis=0)
    scale_a_grad = jnp.sum(attn_grad * normed_a, axis=0)
    latents_low = (one_grad + layer_norm_back(latent_rows, attn_grad * (1.0 + scale_a))).astype(BF)

    local_mod = jnp.stack(
        [shift_a_grad, scale_a_grad, gate_a_grad, shift_m_grad, scale_m_grad, gate_m_grad]
    )
    sums = jnp.concatenate(
        [
            local_mod,
            query_gaingrad,
            key_gaingrad,
            normgain_grad[None],
            normbias_grad[None],
            crossq_gaingrad,
            crossk_gaingrad,
        ]
    )
    for bit in plan.group_bits:
        sums = sums + plan.over_seq(sums, bit)
    other_sums = plan.over_seq(sums, plan.half)
    both_low = jnp.stack([layer_low, latents_low])
    both_low, key_sum, value_sum, query_sum = together(both_low, key_sum, value_sum, query_sum)
    half_rows = both_low.shape[1] // 2
    both_sent = plan.over_seq(both_low[:, half_rows:], plan.half)
    layer_output, latents_gradient = [
        jnp.where(plan.top == 0, jnp.stack([own, other]), jnp.stack([other, own]))
        for own, other in zip(both_low[:, :half_rows], both_sent)
    ]
    latents_gradient = latents_gradient.astype(F32)
    key_sum = plan.scatter_dps(key_sum, xy[1:], (xy[0],))
    value_sum = plan.scatter_dps(value_sum, yx[1:], (yx[0],))
    selfquery_gradient = plan.scatter_last(query_sum)
    up_pieces = [plan.pick(up_term, plan.dp ^ j, 0) for j in range(dp_n)]
    up_pieces = [plan.over_dp(one, j) if j else one for j, one in enumerate(up_pieces)]
    upmatrix_gradient = jnp.concatenate(plan.xor_order(up_pieces, plan.dp), axis=1).astype(F32)
    key_sum, value_sum = together(key_sum, value_sum)
    selfkey_gradient, selfvalue_gradient = plan.scatter_last(key_sum), plan.scatter_last(value_sum)
    modulation_gradient = jnp.where(
        plan.top == 0, jnp.stack([sums[:6], other_sums[:6]]), jnp.stack([other_sums[:6], sums[:6]])
    )
    sums = sums + other_sums
    for bit in plan.dp_bits:
        sums = sums + plan.over_dp(sums, bit)
    small_grads = lax.dynamic_index_in_dim(
        sums.reshape(12, plan.total, shard_rows), plan.me, 1, keepdims=False
    )
    return (
        layer_output,
        latents_gradient,
        context_gradient.astype(F32),
        modulation_gradient,
        small_grads[:6],
        selfquery_gradient,
        selfkey_gradient,
        selfvalue_gradient,
        selfout_gradient,
        small_grads[6],
        small_grads[7],
        small_grads[8],
        small_grads[9],
        crossquery_gradient,
        text_gradients[:, :width],
        text_gradients[:, width:],
        crossout_gradient,
        small_grads[10],
        small_grads[11],
        upmatrix_gradient,
        downmatrix_gradient,
    )


def solution(mesh):
    tokens = P("dp", "seq", None)
    clip = P("dp", None, None)
    table = P(None, ("dp", "seq"))
    matrix = P(("dp", "seq"), None)
    gain = P(("dp", "seq"))
    weights = (matrix,) * 4 + (gain,) * 4 + (matrix,) * 4 + (gain,) * 2 + (matrix,) * 2
    return jax.shard_map(
        functools.partial(body, Plan(mesh)),
        mesh=mesh,
        in_specs=(tokens, tokens, clip, tokens, table) + weights,
        out_specs=(tokens, tokens, tokens, clip, table) + weights,
        check_vma=False,
    )
```

```python
import functools
import math

import jax
import jax.numpy as jnp
import numpy as np
from jax import lax
from jax.experimental import pallas as pl
from jax.experimental.pallas import tpu as pltpu
from jax.sharding import PartitionSpec as P

HEADS = 12
HEAD_DIM = 128
GRID_H = 32
GRID_W = 32
EPS = 1e-06
BF = jnp.bfloat16
F32 = jnp.float32
SCALE = HEAD_DIM ** (-0.5)
SCALE_LOG2 = SCALE * math.log2(math.e)


def layer_norm(values):
    center = values - jnp.mean(values, axis=-1, keepdims=True)
    return center * lax.rsqrt(jnp.mean(center * center, axis=-1, keepdims=True) + EPS)


def layer_norm_back(values, gradient):
    center = values - jnp.mean(values, axis=-1, keepdims=True)
    inverse = lax.rsqrt(jnp.mean(center * center, axis=-1, keepdims=True) + EPS)
    normed = center * inverse
    return inverse * (
        gradient
        - jnp.mean(gradient, axis=-1, keepdims=True)
        - normed * jnp.mean(gradient * normed, axis=-1, keepdims=True)
    )


def gelu_tanh(values):
    return jax.nn.gelu(values, approximate=True)


def dot_nn(left, right, out=F32):
    return lax.dot_general(left, right, (((1,), (0,)), ((), ())), preferred_element_type=F32).astype(out)


def dot_nt(left, right, out=F32):
    return lax.dot_general(left, right, (((1,), (1,)), ((), ())), preferred_element_type=F32).astype(out)


def dot_tn(left, right, out=F32):
    return lax.dot_general(left, right, (((0,), (0,)), ((), ())), preferred_element_type=F32).astype(out)


def rotary_tables(positions):
    pairs = HEAD_DIM // 2
    side = pairs // 3
    lead = pairs - 2 * side

    def rates(number):
        return np.power(np.float32(10000.0), -np.arange(number, dtype=np.float32) / np.float32(number))

    def lanes(start, values):
        row = np.zeros((pairs,), np.float32)
        row[start : start + len(values)] = values
        return np.repeat(row, 2)[None]

    frame = (positions // (GRID_H * GRID_W)).astype(F32)[:, None]
    line = (positions // GRID_W % GRID_H).astype(F32)[:, None]
    column = (positions % GRID_W).astype(F32)[:, None]
    angles = (
        frame * lanes(0, rates(lead))
        + line * lanes(lead, rates(side))
        + column * lanes(lead + side, rates(side))
    )
    even = (np.arange(HEAD_DIM) % 2 == 0)[None]
    sine = jnp.sin(angles)
    return jnp.cos(angles), jnp.where(even, -sine, 0.0), jnp.where(even, 0.0, sine)


def turn(values, cosine, following, previous):
    return (
        values * cosine
        + pltpu.roll(values, HEAD_DIM - 1, 1) * following
        + pltpu.roll(values, 1, 1) * previous
    )


def head_lanes(head):
    return slice(head * HEAD_DIM, (head + 1) * HEAD_DIM)


def row_block(rows):
    return 128 if rows % 128 == 0 else rows


def row_spec(block, width):
    return pl.BlockSpec((block, width), lambda step: (step, 0))


def fixed_spec(width):
    return pl.BlockSpec((1, width), lambda step: (0, 0))


def params(mebibytes):
    return pltpu.CompilerParams(vmem_limit_bytes=mebibytes * 2**20)


def normed_turned(raw_ref, gain_ref, tables, write):
    raw = raw_ref[...]
    inverse = lax.rsqrt(jnp.mean(raw * raw, axis=-1, keepdims=True) + EPS)
    normed = raw * inverse * gain_ref[...]
    for head in range(HEADS):
        piece = normed[:, head_lanes(head)]
        if tables is not None:
            piece = turn(piece, *tables)
        write(head, piece.astype(BF))


def self_post(raw, gain_query, gain_key, tables, groups):
    rows, width = raw.shape[0], raw.shape[1] // 3
    block = row_block(rows)
    per_group = HEADS // groups

    def kernel(query_ref, key_ref, value_ref, gq_ref, gk_ref, cos_ref, next_ref, last_ref, query_out, *outs):
        turns = (cos_ref[...], next_ref[...], last_ref[...])

        def write_query(head, piece):
            query_out[:, head_lanes(head)] = piece

        def write_key(head, piece):
            start = (head % per_group) * 2 * HEAD_DIM
            outs[head // per_group][:, start : start + HEAD_DIM] = piece

        normed_turned(query_ref, gq_ref, turns, write_query)
        normed_turned(key_ref, gk_ref, turns, write_key)
        for head in range(HEADS):
            start = (head % per_group) * 2 * HEAD_DIM + HEAD_DIM
            outs[head // per_group][:, start : start + HEAD_DIM] = value_ref[:, head_lanes(head)].astype(BF)

    out_width = per_group * 2 * HEAD_DIM
    return pl.pallas_call(
        kernel,
        grid=(rows // block,),
        in_specs=[pl.BlockSpec((block, width), lambda step, part=part: (step, part)) for part in range(3)]
        + [fixed_spec(width)] * 2
        + [row_spec(block, HEAD_DIM)] * 3,
        out_specs=[row_spec(block, width)] + [row_spec(block, out_width)] * groups,
        out_shape=[jax.ShapeDtypeStruct((rows, width), BF)]
        + [jax.ShapeDtypeStruct((rows, out_width), BF)] * groups,
        compiler_params=params(32),
        cost_estimate=pl.CostEstimate(flops=rows * width * 20, bytes_accessed=rows * width * 18, transcendentals=0),
        name="self_post",
    )(raw, raw, raw, gain_query, gain_key, *tables)


def query_post(raw, gain):
    rows, width = raw.shape
    block = row_block(rows)

    def kernel(raw_ref, gain_ref, out_ref):
        def write(head, piece):
            out_ref[:, head_lanes(head)] = piece

        normed_turned(raw_ref, gain_ref, None, write)

    return pl.pallas_call(
        kernel,
        grid=(rows // block,),
        in_specs=[row_spec(block, width), fixed_spec(width)],
        out_specs=row_spec(block, width),
        out_shape=jax.ShapeDtypeStruct((rows, width), BF),
        compiler_params=params(24),
        cost_estimate=pl.CostEstimate(flops=rows * width * 10, bytes_accessed=rows * width * 6, transcendentals=0),
        name="query_post",
    )(raw, gain)


def text_post(raw, gain):
    rows, width = raw.shape[0], raw.shape[1] // 2
    block = row_block(rows)

    def kernel(key_ref, value_ref, gain_ref, out_ref):
        def write(head, piece):
            out_ref[:, 2 * head * HEAD_DIM : (2 * head + 1) * HEAD_DIM] = piece

        normed_turned(key_ref, gain_ref, None, write)
        for head in range(HEADS):
            start = (2 * head + 1) * HEAD_DIM
            out_ref[:, start : start + HEAD_DIM] = value_ref[:, head_lanes(head)].astype(BF)

    return pl.pallas_call(
        kernel,
        grid=(rows // block,),
        in_specs=[pl.BlockSpec((block, width), lambda step, part=part: (step, part)) for part in range(2)]
        + [fixed_spec(width)],
        out_specs=row_spec(block, 2 * width),
        out_shape=jax.ShapeDtypeStruct((rows, 2 * width), BF),
        compiler_params=params(24),
        cost_estimate=pl.CostEstimate(flops=rows * width * 10, bytes_accessed=rows * width * 12, transcendentals=0),
        name="text_post",
    )(raw, raw, gain)


def norm_back(raw, gain, gradient):
    inverse = lax.rsqrt(jnp.mean(raw * raw, axis=-1, keepdims=True) + EPS)
    normed = raw * inverse
    gained = gradient * gain
    back = (gained - normed * jnp.mean(gained * normed, axis=-1, keepdims=True)) * inverse
    return back, jnp.sum(gradient * normed, axis=0, keepdims=True)


def turned_back(piece, turns):
    return piece if turns is None else turn(piece, turns[0], -turns[1], -turns[2])


def accumulate(ref, term):
    @pl.when(pl.program_id(0) == 0)
    def _():
        ref[...] = jnp.zeros_like(ref)

    ref[...] += term


def self_query_back(gradients, raw, gain, tables):
    rows, width = raw.shape[0], raw.shape[1] // 3
    block = row_block(rows)
    groups = len(gradients)
    per_group = HEADS // groups

    def kernel(*refs):
        grads = refs[:groups]
        raw_ref, gain_ref, cos_ref, next_ref, last_ref, low_ref, gain_out = refs[groups:]
        turns = (cos_ref[...], next_ref[...], last_ref[...])
        pieces = [
            turned_back(grads[head // per_group][:, head_lanes(head % per_group)], turns)
            for head in range(HEADS)
        ]
        back, term = norm_back(raw_ref[...], gain_ref[...], jnp.concatenate(pieces, axis=1))
        low_ref[...] = back.astype(BF)
        accumulate(gain_out, term)

    return pl.pallas_call(
        kernel,
        grid=(rows // block,),
        in_specs=[row_spec(block, per_group * HEAD_DIM)] * groups
        + [row_spec(block, width), fixed_spec(width)]
        + [row_spec(block, HEAD_DIM)] * 3,
        out_specs=[row_spec(block, width), fixed_spec(width)],
        out_shape=[jax.ShapeDtypeStruct((rows, width), BF), jax.ShapeDtypeStruct((1, width), F32)],
        compiler_params=params(32),
        cost_estimate=pl.CostEstimate(flops=rows * width * 15, bytes_accessed=rows * width * 10, transcendentals=0),
        name="self_query_back",
    )(*gradients, raw, gain, *tables)


def self_keyvalue_back(gradients, raw, gain, tables):
    rows, width = raw.shape[0], raw.shape[1] // 3
    block = row_block(rows)
    groups = len(gradients)
    per_group = HEADS // groups

    def kernel(*refs):
        grads = refs[:groups]
        raw_ref, gain_ref, cos_ref, next_ref, last_ref, low_ref, gain_out = refs[groups:]
        turns = (cos_ref[...], next_ref[...], last_ref[...])
        pieces = []
        for head in range(HEADS):
            start = (head % per_group) * 2 * HEAD_DIM
            ref = grads[head // per_group]
            pieces.append(turned_back(ref[:, start : start + HEAD_DIM], turns))
            value = ref[:, start + HEAD_DIM : start + 2 * HEAD_DIM].astype(BF)
            low_ref[:, width + head * HEAD_DIM : width + (head + 1) * HEAD_DIM] = value
        back, term = norm_back(raw_ref[...], gain_ref[...], jnp.concatenate(pieces, axis=1))
        low_ref[:, :width] = back.astype(BF)
        accumulate(gain_out, term)

    return pl.pallas_call(
        kernel,
        grid=(rows // block,),
        in_specs=[row_spec(block, per_group * 2 * HEAD_DIM)] * groups
        + [pl.BlockSpec((block, width), lambda step: (step, 1)), fixed_spec(width)]
        + [row_spec(block, HEAD_DIM)] * 3,
        out_specs=[row_spec(block, 2 * width), fixed_spec(width)],
        out_shape=[jax.ShapeDtypeStruct((rows, 2 * width), BF), jax.ShapeDtypeStruct((1, width), F32)],
        compiler_params=params(32),
        cost_estimate=pl.CostEstimate(flops=rows * width * 15, bytes_accessed=rows * width * 18, transcendentals=0),
        name="self_keyvalue_back",
    )(*gradients, raw, gain, *tables)


def query_back(gradient, raw, gain):
    rows, width = raw.shape
    block = row_block(rows)

    def kernel(grad_ref, raw_ref, gain_ref, low_ref, gain_out):
        back, term = norm_back(raw_ref[...], gain_ref[...], grad_ref[...])
        low_ref[...] = back.astype(BF)
        accumulate(gain_out, term)

    return pl.pallas_call(
        kernel,
        grid=(rows // block,),
        in_specs=[row_spec(block, width), row_spec(block, width), fixed_spec(width)],
        out_specs=[row_spec(block, width), fixed_spec(width)],
        out_shape=[jax.ShapeDtypeStruct((rows, width), BF), jax.ShapeDtypeStruct((1, width), F32)],
        compiler_params=params(24),
        cost_estimate=pl.CostEstimate(flops=rows * width * 15, bytes_accessed=rows * width * 10, transcendentals=0),
        name="query_back",
    )(gradient, raw, gain)


def text_back(gradient, raw, gain):
    rows, width = raw.shape[0], raw.shape[1] // 2
    block = row_block(rows)

    def kernel(grad_ref, raw_ref, gain_ref, low_ref, gain_out):
        pieces = []
        for head in range(HEADS):
            start = 2 * head * HEAD_DIM
            pieces.append(grad_ref[:, start : start + HEAD_DIM])
            value = grad_ref[:, start + HEAD_DIM : start + 2 * HEAD_DIM].astype(BF)
            low_ref[:, width + head * HEAD_DIM : width + (head + 1) * HEAD_DIM] = value
        back, term = norm_back(raw_ref[...], gain_ref[...], jnp.concatenate(pieces, axis=1))
        low_ref[:, :width] = back.astype(BF)
        accumulate(gain_out, term)

    return pl.pallas_call(
        kernel,
        grid=(rows // block,),
        in_specs=[row_spec(block, 2 * width), row_spec(block, width), fixed_spec(width)],
        out_specs=[row_spec(block, 2 * width), fixed_spec(width)],
        out_shape=[jax.ShapeDtypeStruct((rows, 2 * width), BF), jax.ShapeDtypeStruct((1, width), F32)],
        compiler_params=params(24),
        cost_estimate=pl.CostEstimate(flops=rows * width * 15, bytes_accessed=rows * width * 16, transcendentals=0),
        name="text_back",
    )(gradient, raw, gain)


def attend(query, chunks, base, heads):
    rows = query.shape[0]
    count = len(chunks)
    keys = chunks[0].shape[0]

    def kernel(query_ref, *refs):
        out_ref, log_ref = refs[count:]
        query_head = query_ref[...]
        scores = [dot_nt(ref[:, :HEAD_DIM], query_head) for ref in refs[:count]]
        peak = functools.reduce(
            jnp.maximum, [jnp.max(score, axis=0, keepdims=True) for score in scores]
        )
        shift = peak * SCALE_LOG2
        total = jnp.zeros((1, rows), F32)
        summed = jnp.zeros((HEAD_DIM, rows), F32)
        for ref, score in zip(refs[:count], scores):
            weight = jnp.exp2(score * SCALE_LOG2 - shift)
            total += jnp.sum(weight, axis=0, keepdims=True)
            summed += dot_tn(ref[:, HEAD_DIM:], weight.astype(BF))
        out_ref[...] = (summed / total).T.astype(BF)
        log_ref[0] = shift + jnp.log2(total)

    return pl.pallas_call(
        kernel,
        grid=(heads,),
        in_specs=[pl.BlockSpec((rows, HEAD_DIM), lambda head: (0, base + head))]
        + [pl.BlockSpec((keys, 2 * HEAD_DIM), lambda head: (0, head))] * count,
        out_specs=[
            pl.BlockSpec((rows, HEAD_DIM), lambda head: (0, head)),
            pl.BlockSpec((1, 1, rows), lambda head: (head, 0, 0)),
        ],
        out_shape=[
            jax.ShapeDtypeStruct((rows, heads * HEAD_DIM), BF),
            jax.ShapeDtypeStruct((heads, 1, rows), F32),
        ],
        compiler_params=params(40),
        cost_estimate=pl.CostEstimate(
            flops=heads * rows * keys * count * HEAD_DIM * 4 * 2,
            bytes_accessed=heads * HEAD_DIM * 2 * (2 * rows + 2 * keys * count),
            transcendentals=heads * rows * keys * count,
        ),
        name="attend",
    )(query, *chunks)


def attend_back(query, chunks, gradient, logs, base, heads):
    rows = query.shape[0]
    count = len(chunks)
    keys = chunks[0].shape[0]

    def kernel(query_ref, grad_ref, log_ref, *refs):
        query_grad = refs[count]
        query_head, grad_head = query_ref[...], grad_ref[...]
        shift = log_ref[0]
        weights, value_grads = [], []
        delta = jnp.zeros((1, rows), F32)
        for ref in refs[:count]:
            weight = jnp.exp2(dot_nt(ref[:, :HEAD_DIM], query_head) * SCALE_LOG2 - shift)
            value_grad = dot_nt(ref[:, HEAD_DIM:], grad_head)
            delta += jnp.sum(weight * value_grad, axis=0, keepdims=True)
            weights.append(weight)
            value_grads.append(value_grad)
        summed = jnp.zeros((HEAD_DIM, rows), F32)
        for ref, out, weight, value_grad in zip(refs[:count], refs[count + 1 :], weights, value_grads):
            score_grad = (weight * (value_grad - delta)).astype(BF)
            out[:, :HEAD_DIM] = (dot_nn(score_grad, query_head) * SCALE).astype(BF)
            out[:, HEAD_DIM:] = dot_nn(weight.astype(BF), grad_head).astype(BF)
            summed += dot_tn(ref[:, :HEAD_DIM], score_grad)
        query_grad[...] = (summed * SCALE).T

    return pl.pallas_call(
        kernel,
        grid=(heads,),
        in_specs=[
            pl.BlockSpec((rows, HEAD_DIM), lambda head: (0, base + head)),
            pl.BlockSpec((rows, HEAD_DIM), lambda head: (0, base + head)),
            pl.BlockSpec((1, 1, rows), lambda head: (head, 0, 0)),
        ]
        + [pl.BlockSpec((keys, 2 * HEAD_DIM), lambda head: (0, head))] * count,
        out_specs=[pl.BlockSpec((rows, HEAD_DIM), lambda head: (0, head))]
        + [pl.BlockSpec((keys, 2 * HEAD_DIM), lambda head: (0, head))] * count,
        out_shape=[jax.ShapeDtypeStruct((rows, heads * HEAD_DIM), F32)]
        + [jax.ShapeDtypeStruct((keys, heads * 2 * HEAD_DIM), BF)] * count,
        compiler_params=params(40),
        cost_estimate=pl.CostEstimate(
            flops=heads * rows * keys * count * HEAD_DIM * 10 * 2,
            bytes_accessed=heads * HEAD_DIM * 2 * (5 * rows + 4 * keys * count),
            transcendentals=heads * rows * keys * count,
        ),
        name="attend_back",
    )(query, gradient, logs, *chunks)


def place_rows(numbers, left, right, rows, total):
    slots, _, right_width = right[0][0].shape
    left_width = left[0][0].shape[2]
    count = len(left)
    extra = left_width > right_width

    def kernel(numbers_ref, *refs):
        whole_ref = refs[4 * count]
        step = pl.program_id(0)
        for at in range(count):
            for core in range(2):

                @pl.when((step // slots == at) & (numbers_ref[0] == core))
                def _():
                    for other in range(2):
                        place = pl.ds((other ^ core) * rows, rows)
                        left_ref, right_ref = refs[4 * at + other], refs[4 * at + 2 + other]
                        whole_ref[place, :right_width] = left_ref[0, :, :right_width]
                        whole_ref[place, right_width:] = right_ref[0]
                        if extra:
                            refs[4 * count + 1][place] = left_ref[0, :, right_width:]

    def source(at, width):
        return pl.BlockSpec(
            (1, rows, width),
            lambda step, numbers_ref: (jnp.clip(step - at * slots, 0, slots - 1), 0, 0),
        )

    def index(step, numbers_ref):
        return (numbers_ref[step + 1], 0)

    in_specs, arrays = [], []
    for at in range(count):
        in_specs += [source(at, left_width)] * 2 + [source(at, right_width)] * 2
        arrays += [*left[at], *right[at]]
    return pl.pallas_call(
        kernel,
        grid_spec=pltpu.PrefetchScalarGridSpec(
            num_scalar_prefetch=1,
            grid=(count * slots,),
            in_specs=in_specs,
            out_specs=[
                pl.BlockSpec((2 * rows, 2 * right_width), index),
                pl.BlockSpec((2 * rows, left_width - right_width), index),
            ][: 1 + extra],
        ),
        out_shape=[
            jax.ShapeDtypeStruct((total, 2 * right_width), BF),
            jax.ShapeDtypeStruct((total, left_width - right_width), BF),
        ][: 1 + extra],
        compiler_params=params(32),
        cost_estimate=pl.CostEstimate(flops=0, bytes_accessed=8 * total * right_width, transcendentals=0),
        name="place_rows",
    )(numbers, *arrays)


def after(value, *others):
    return lax.optimization_barrier((value,) + others)[0]


def together(*values):
    return lax.optimization_barrier(values)


class Plan:
    def __init__(self, mesh):
        self.dp_n = mesh.shape["dp"]
        self.seq_n = mesh.shape["seq"]
        self.total = self.dp_n * self.seq_n
        self.half = self.seq_n // 2
        self.columns = self.seq_n // 2
        self.groups = 3 if self.half <= 4 else 1
        self.dp_bits = [1 << i for i in range(self.dp_n.bit_length() - 1)]
        self.group_bits = [1 << i for i in range(self.half.bit_length() - 1)]

    def start(self):
        self.dp = lax.axis_index("dp")
        self.seq = lax.axis_index("seq")
        self.me = self.dp * self.seq_n + self.seq
        self.core = self.seq % 2
        self.column = self.seq // 2
        self.top = self.seq // self.half

    def over_seq(self, value, offset):
        return lax.ppermute(value, "seq", [(i, i ^ offset) for i in range(self.seq_n)])

    def over_dp(self, value, offset):
        return lax.ppermute(value, "dp", [(i, i ^ offset) for i in range(self.dp_n)])


    def shift(self, value):
        own = lax.dynamic_index_in_dim(value, self.top, 0, keepdims=False)
        other = lax.dynamic_index_in_dim(value, 1 - self.top, 0, keepdims=False)
        return jnp.concatenate([own, self.over_seq(other, self.half)], axis=0)

    def unshift(self, value):
        rows = value.shape[0] // 2
        own, other = value[:rows], self.over_seq(value[rows:], self.half)
        return jnp.where(self.top == 0, jnp.stack([own, other]), jnp.stack([other, own]))


    def group_gather(self, value, *behind):
        held = {0: after(value, *behind) if behind else value}
        for bit in reversed(self.group_bits):
            held.update({at ^ bit: self.over_seq(one, bit) for at, one in list(held.items())})
        return held

    def group_scatter(self, held):
        held = dict(held)
        for bit in self.group_bits:
            for at in sorted(held):
                if at & bit:
                    sent = self.over_seq(held.pop(at).astype(BF), bit)
                    held[at ^ bit] = held[at ^ bit].astype(F32) + sent.astype(F32)
        return held[0]


    def gather_columns(self, shard):
        return jnp.stack([shard] + [self.over_seq(shard, 2 * k) for k in range(1, self.columns)])

    def gather_dp(self, sides, orders, number):
        return [
            {at ^ order[number]: self.over_dp(one, order[number]) for at, one in side.items()}
            for side, order in zip(sides, orders)
        ]

    def gather_place(self, sides):
        left, right = [{at: (one, self.over_seq(one, 1)) for at, one in side.items()} for side in sides]
        slots = self.columns
        rows, width = right[0][0].shape[1:]
        if rows % 16 == 0:
            blocks = [(self.dp ^ at) * slots + (self.column ^ slot) for at in left for slot in range(slots)]
            numbers = jnp.stack([self.core] + blocks).astype(jnp.int32)
            return place_rows(
                numbers, list(left.values()), [right[at] for at in left], rows, self.total * rows
            )
        wholes = []
        for held in (left, right):
            pieces = [
                held[number // self.seq_n][number % 2][(number % self.seq_n) // 2]
                for number in range(self.total)
            ]
            stacked = jnp.stack(pieces)

            def place(number, out):
                return lax.dynamic_update_index_in_dim(
                    out, self.pick(stacked, number, 0), number ^ self.me, 0
                )

            ordered = lax.fori_loop(0, self.total, place, jnp.zeros_like(stacked))
            wholes.append(ordered.reshape(self.total * rows, -1))
        left, right = wholes
        return [jnp.concatenate([left[:, :width], right], axis=1), left[:, width:]]

    def xor_order(self, pieces, number):
        bit = 1
        while bit < len(pieces):
            swapped = (number // bit) % 2 == 1
            pieces = [jnp.where(swapped, pieces[i ^ bit], pieces[i]) for i in range(len(pieces))]
            bit *= 2
        return pieces

    def pick(self, value, number, axis):
        return lax.dynamic_index_in_dim(value, number, axis, keepdims=False)

    def scatter_columns(self, value, axis, wire):
        total = self.pick(value, self.column, axis).astype(F32)
        for k in range(1, self.columns):
            sent = self.over_seq(self.pick(value, self.column ^ k, axis).astype(wire), 2 * k)
            total = total + sent.astype(F32)
        return total


    def scatter_core(self, *values):
        bits = len(self.dp_bits)
        values = [
            one.reshape((2,) * bits + (self.columns, 2, one.shape[0] // self.total, one.shape[1]))
            for one in values
        ]
        kept, sent = [
            jnp.concatenate([self.pick(one, core, bits + 1) for one in values], axis=-1)
            for core in (self.core, 1 - self.core)
        ]
        return kept, self.over_seq(sent, 1)

    def scatter_dp(self, halves, done, bit):
        value = (halves[0].astype(F32) + halves[1].astype(F32)).astype(BF)
        axis = [one for one in reversed(self.dp_bits) if one not in done].index(bit)
        mine = (self.dp // bit) % 2
        sent = self.over_dp(self.pick(value, 1 - mine, axis), bit)
        return self.pick(value, mine, axis), sent

    def scatter_pair(self, pair, orders, number):
        return [
            self.scatter_dp(halves, order[:number], order[number]) for halves, order in zip(pair, orders)
        ]

    def scatter_pair_last(self, pair):
        value = jnp.concatenate([halves[0].astype(F32) + halves[1].astype(F32) for halves in pair], axis=-1)
        width = pair[0][0].shape[-1]
        total = self.scatter_columns(value.astype(BF), 0, BF)
        return total[:, :width], total[:, width:]


def body(
    plan,
    latents,
    context,
    modulation,
    cotangent,
    modtable,
    selfquery,
    selfkey,
    selfvalue,
    selfout,
    querygain,
    keygain,
    normgain,
    normbias,
    crossquery,
    crosskey,
    crossvalue,
    crossout,
    crossqgain,
    crosskgain,
    upmatrix,
    downmatrix,
):
    plan.start()
    width = latents.shape[2]
    dp_n, seq_n, columns = plan.dp_n, plan.seq_n, plan.columns
    everywhere = ("dp", "seq")
    rows_one = latents.shape[1]
    shard_rows = selfquery.shape[0]
    hidden = upmatrix.shape[1]
    part = hidden // dp_n
    xy, yx = plan.dp_bits, list(reversed(plan.dp_bits))

    small = jnp.concatenate(
        [modtable.T]
        + [gain[:, None] for gain in (querygain, keygain, normgain, normbias, crossqgain, crosskgain)]
        + [jnp.zeros((shard_rows, HEAD_DIM - 12), BF)],
        axis=1,
    )
    middle = 3 * width // 2
    side = jnp.concatenate([selfquery, selfkey, selfvalue], axis=1)
    both = plan.gather_columns(jnp.concatenate([side[:, :middle], small, side[:, middle:]], axis=1))
    token_rows = plan.shift(latents)
    up_parts = [
        lax.dynamic_slice_in_dim(upmatrix, (plan.dp ^ j) * part, part, 1) for j in range(dp_n)
    ]
    up_parts = [plan.over_dp(one, j) if j else one for j, one in enumerate(up_parts)]
    both, token_rows, up_parts = together(both, token_rows, up_parts)
    up_shard = jnp.concatenate(plan.xor_order(up_parts, plan.dp), axis=0)
    edge = middle + HEAD_DIM
    first = [{0: both[:, :, :edge]}, {0: both[:, :, edge:]}]

    others = after(jnp.concatenate([selfout, crossquery, crossout, crosskey, crossvalue], axis=1), both)
    others = plan.gather_columns(others)
    for number in range(len(xy)):
        arrived = plan.gather_dp(first, (xy, yx), number)
        if number + 1 < len(xy):
            arrived = together(*arrived)
        else:
            *arrived, others = together(*arrived, others)
        first = [{**side, **more} for side, more in zip(first, arrived)]
    whole_self, small_all = plan.gather_place(first)
    small_placed = small_all
    small_all = small_all.T[:12].astype(F32)
    edge = 5 * width // 2
    second = [{0: others[:, :, :edge]}, {0: others[:, :, edge:]}]

    mod_rows = lax.dynamic_index_in_dim(modulation, plan.top, 0, keepdims=False) + small_all[:6]
    shift_a, scale_a, gate_a, shift_m, scale_m, gate_m = [mod_rows[i : i + 1] for i in range(6)]
    gain_query, gain_key, gain_norm, bias_norm, gain_crossq, gain_crossk = [
        small_all[i : i + 1] for i in range(6, 12)
    ]
    span = jnp.arange(rows_one, dtype=jnp.int32)
    positions = jnp.concatenate(
        [plan.seq * rows_one + span, (plan.seq ^ plan.half) * rows_one + span]
    )
    tables = rotary_tables(positions)

    latent_rows = token_rows.astype(F32)
    normed_a = layer_norm(latent_rows)
    attn_in = (normed_a * (1.0 + scale_a) + shift_a).astype(BF)
    self_raw = dot_nn(attn_in, whole_self)
    shifted = plan.shift(after(jnp.concatenate([cotangent, context], axis=1), small_placed))
    *arrived, self_raw = together(*plan.gather_dp(second, (xy, yx), 0), self_raw)
    second = [{**side, **more} for side, more in zip(second, arrived)]
    queries, *keyvalues = self_post(self_raw, gain_query, gain_key, tables, plan.groups)
    keyvalues, shifted = together(keyvalues, shifted)
    text_one = context.shape[1]
    step = rows_one + text_one
    grad_rows = jnp.concatenate([shifted[:rows_one], shifted[step : step + rows_one]])
    text_rows = jnp.concatenate([shifted[rows_one:step], shifted[step + rows_one :]])
    per_group = HEADS // plan.groups
    gathered = []
    for group, one in enumerate(keyvalues):
        behind = [gathered[-1][plan.group_bits[-1]]] if gathered else []
        gathered.append(plan.group_gather(one, *behind))
        if group < 2:
            number = len(xy) - 1
            if group == 0:
                for early in range(1, number):
                    arrived = plan.gather_dp(second, (xy, yx), early)
                    second = [{**side, **more} for side, more in zip(second, arrived)]
                half = len(second[0]) // 2
                parts = [dict(list(side.items())[:half]) for side in second]
                whole_second = [dict(side) for side in second]
            else:
                parts = [dict(list(side.items())[half:]) for side in second]
                parts, arrived = together(parts, arrived)
            if plan.groups == 1:
                parts = second
            bit = plan.group_bits[-1]
            arrived, gathered[-1][bit] = together(
                plan.gather_dp(parts, (xy, yx), number), gathered[-1][bit]
            )
            whole_second = [{**side, **more} for side, more in zip(whole_second, arrived)]
    second = whole_second
    arrived = gathered[-1][plan.group_bits[-1]]
    (whole_others,) = plan.gather_place(second)[:1]
    whole_selfout, whole_crossquery, whole_crossout = [
        whole_others[:, i * width : (i + 1) * width] for i in range(3)
    ]
    whole_crosstext = whole_others[:, 3 * width :]
    text_raw = dot_nn(text_rows, whole_crosstext)
    text_keyvalues = text_post(text_raw, gain_crossk)
    gathered[-1], text_keyvalues = together(gathered[-1], text_keyvalues)
    cross_gathered = plan.group_gather(text_keyvalues)
    up_shard = after(up_shard, arrived)
    whole_up = lax.all_gather(up_shard, "seq", axis=0, tiled=True)
    whole_up = (
        whole_up.reshape(seq_n, dp_n, shard_rows, part)
        .transpose(1, 0, 2, 3)
        .reshape(plan.total * shard_rows, part)
    )
    self_outs, self_logs = [], []
    for group in range(plan.groups):
        out, logs = attend(queries, list(gathered[group].values()), group * per_group, per_group)
        self_outs.append(out)
        self_logs.append(logs)
    down_shard = after(downmatrix, cross_gathered[plan.group_bits[-1]])
    whole_down = lax.all_gather(down_shard, "seq", axis=0, tiled=True)
    out_grad = grad_rows.astype(F32)
    down_grad = (out_grad * gate_m).astype(BF)
    down_grads = [down_grad] + [plan.over_dp(down_grad, j) for j in range(1, dp_n)]
    attended = jnp.concatenate(self_outs, axis=1)
    self_branch = dot_nn(attended, whole_selfout)
    hidden_one = latent_rows + self_branch * gate_a

    cross_in = (layer_norm(hidden_one) * gain_norm + bias_norm).astype(BF)
    crossq_raw = dot_nn(cross_in, whole_crossquery)
    cross_queries = query_post(crossq_raw, gain_crossq)
    crossed, cross_logs = attend(cross_queries, list(cross_gathered.values()), 0, HEADS)
    crossed, down_grads = together(crossed, down_grads)
    hidden_two = hidden_one + dot_nn(crossed, whole_crossout)

    normed_m = layer_norm(hidden_two)
    mlp_in = (normed_m * (1.0 + scale_m) + shift_m).astype(BF)
    received = [plan.over_dp(mlp_in, j) for j in range(1, dp_n)]
    mlp_ins, activations, up_grads, mlp_grads = [mlp_in], [], [], []
    for j in range(dp_n):
        up_values = dot_nn(mlp_ins[j], whole_up)
        activation, gelu_back = jax.vjp(gelu_tanh, up_values)
        activations.append(activation.astype(BF))
        up_grads.append(gelu_back(dot_nt(down_grads[j], whole_down))[0].astype(BF))
        mlp_grads.append(dot_nt(up_grads[j], whole_up, BF if j else F32))
        if j + 1 < dp_n:
            one, activations[j] = together(received[j], activations[j])
            mlp_ins.append(one)
    mlp_sent = [plan.over_dp(mlp_grads[j], j) for j in range(1, dp_n)]

    up_in, down_in, _ = together(jnp.concatenate(mlp_ins), jnp.concatenate(activations), mlp_grads[0])
    down_term = dot_tn(down_in, jnp.concatenate(down_grads), BF)
    up_term = dot_tn(up_in, jnp.concatenate(up_grads), BF)
    up_term = (
        up_term.reshape(dp_n, seq_n, shard_rows, part)
        .transpose(1, 0, 2, 3)
        .reshape(plan.total * shard_rows, part)
    )
    mlp_sent, up_term = together(mlp_sent, up_term)
    downmatrix_gradient = lax.psum_scatter(down_term, "seq", scatter_dimension=0, tiled=True).astype(F32)
    up_term = lax.psum_scatter(up_term, "seq", scatter_dimension=0, tiled=True)
    up_term = up_term.reshape(dp_n, shard_rows, part)
    mlp_grad = mlp_grads[0] + sum(one.astype(F32) for one in mlp_sent)
    activations, mlp_grad = together(activations, mlp_grad)
    down_all = [dot_nn(activations[j], whole_down, BF if j else F32) for j in range(dp_n)]
    down_sent = [plan.over_dp(down_all[j], j) for j in range(1, dp_n)]
    mlp_grad, down_all = together(mlp_grad, down_all)

    shift_m_grad = jnp.sum(mlp_grad, axis=0)
    scale_m_grad = jnp.sum(mlp_grad * normed_m, axis=0)
    two_grad = out_grad + layer_norm_back(hidden_two, mlp_grad * (1.0 + scale_m))
    cross_grad = two_grad.astype(BF)
    crossed_grad = dot_nt(cross_grad, whole_crossout, BF)
    crossout_term = dot_tn(crossed, cross_grad, BF)
    crossq_grad, *cross_parts = attend_back(
        cross_queries, list(cross_gathered.values()), crossed_grad, cross_logs, 0, HEADS
    )
    cross_own = plan.group_scatter(dict(zip(cross_gathered, cross_parts)))
    crossq_low, crossq_gaingrad = query_back(crossq_grad, crossq_raw, gain_crossq)
    cross_sums = [plan.scatter_core(crossout_term), plan.scatter_core(dot_tn(cross_in, crossq_low, BF))]
    crossin_grad = dot_nt(crossq_low, whole_crossquery)
    normgain_grad = jnp.sum(crossin_grad * layer_norm(hidden_one), axis=0)
    normbias_grad = jnp.sum(crossin_grad, axis=0)
    one_grad = two_grad + layer_norm_back(hidden_one, crossin_grad * gain_norm)
    gate_a_grad = jnp.sum(one_grad * self_branch, axis=0)
    branch_grad = (one_grad * gate_a).astype(BF)
    branch_grad, cross_sums = together(branch_grad, cross_sums)
    cross_sums = plan.scatter_pair(cross_sums, (xy, yx), 0)
    attended_grad = dot_nt(branch_grad, whole_selfout, BF)
    query_grads, keyvalue_grads = [], []
    for group in range(plan.groups):
        query_grad, *parts = attend_back(
            queries,
            list(gathered[group].values()),
            attended_grad,
            self_logs[group],
            group * per_group,
            per_group,
        )
        if group == 0:
            query_grad, cross_own = together(query_grad, cross_own)
            text_low, crossk_gaingrad = text_back(cross_own, text_raw, gain_crossk)
            text_term = dot_tn(text_rows, text_low, BF)
            selfout_term = dot_tn(attended, branch_grad, BF)
            pieces = [
                (text_term[:, :width], selfout_term[:, : width // 2]),
                (text_term[:, width:], selfout_term[:, width // 2 :]),
            ]
            text_sums = [plan.scatter_core(*pair) for pair in pieces]
            context_gradient = plan.unshift(dot_nt(text_low, whole_crosstext, BF))
        if group == min(1, plan.groups - 1):
            query_grad, cross_sums, text_sums, context_gradient, down_sent = together(
                query_grad, cross_sums, text_sums, context_gradient, down_sent
            )
            down_values = down_all[0] + sum(one.astype(F32) for one in down_sent)
            layer_output = plan.unshift((hidden_two + down_values * gate_m).astype(BF))
            gate_m_grad = jnp.sum(out_grad * down_values, axis=0)
            for number in range(1, len(xy)):
                cross_sums = plan.scatter_pair(cross_sums, (xy, yx), number)
            text_sums = plan.scatter_pair(text_sums, (xy, yx), 0)
        if group == plan.groups - 1:
            query_grad, cross_sums, text_sums, layer_output = together(
                query_grad, cross_sums, text_sums, layer_output
            )
            for number in range(1, len(xy)):
                text_sums = plan.scatter_pair(text_sums, (xy, yx), number)
            crossout_gradient, crossquery_gradient = plan.scatter_pair_last(cross_sums)
        query_grads.append(query_grad)
        keyvalue_grads.append(plan.group_scatter(dict(zip(gathered[group], parts))))

    query_low, query_gaingrad = self_query_back(query_grads, self_raw, gain_query, tables)
    query_low, text_sums, crossout_gradient, crossquery_gradient = together(
        query_low, text_sums, crossout_gradient, crossquery_gradient
    )
    left, right = plan.scatter_pair_last(text_sums)
    query_term = dot_tn(attn_in, query_low, BF)
    attn_grad = dot_nt(query_low, whole_self[:, :width])
    keyvalue_grads, attn_grad, query_term = together(keyvalue_grads, attn_grad, query_term)
    keyvalue_low, key_gaingrad = self_keyvalue_back(keyvalue_grads, self_raw, gain_key, tables)
    keyvalue_low, left, right = together(keyvalue_low, left, right)
    key_middle = middle - width
    left_term = dot_tn(attn_in, keyvalue_low[:, :key_middle], BF)
    right_term = dot_tn(attn_in, keyvalue_low[:, key_middle:], BF)
    self_sums = [
        plan.scatter_core(query_term, left_term),
        plan.scatter_core(right_term),
    ]
    kept_low, _ = together(keyvalue_low, (left_term, right_term))
    attn_grad = attn_grad + dot_nt(kept_low, whole_self[:, width:])
    attn_grad, self_sums = together(attn_grad, self_sums)
    crosskey_gradient, crossvalue_gradient = left[:, :width], right[:, :width]
    selfout_gradient = jnp.concatenate([left[:, width:], right[:, width:]], axis=1)
    self_sums = plan.scatter_pair(self_sums, (xy, yx), 0)
    shift_a_grad = jnp.sum(attn_grad, axis=0)
    scale_a_grad = jnp.sum(attn_grad * normed_a, axis=0)
    latents_low = (one_grad + layer_norm_back(latent_rows, attn_grad * (1.0 + scale_a))).astype(BF)
    local_mod = jnp.stack(
        [shift_a_grad, scale_a_grad, gate_a_grad, shift_m_grad, scale_m_grad, gate_m_grad]
    )
    sums = jnp.concatenate(
        [
            local_mod,
            query_gaingrad,
            key_gaingrad,
            normgain_grad[None],
            normbias_grad[None],
            crossq_gaingrad,
            crossk_gaingrad,
        ]
    )
    for bit in plan.group_bits:
        sums = sums + plan.over_seq(sums, bit)
    other_sums = plan.over_seq(sums, plan.half)
    latents_low, other_sums = together(latents_low, other_sums)
    latents_gradient = plan.unshift(latents_low)
    for number in range(1, len(xy)):
        self_sums = plan.scatter_pair(self_sums, (xy, yx), number)
    self_sums, latents_gradient = together(self_sums, latents_gradient)
    latents_gradient = latents_gradient.astype(F32)
    self_gradients = jnp.concatenate(plan.scatter_pair_last(together(*self_sums)), axis=1)
    up_pieces = [plan.pick(up_term, plan.dp ^ j, 0) for j in range(dp_n)]
    up_pieces = [plan.over_dp(one, j) if j else one for j, one in enumerate(up_pieces)]
    upmatrix_gradient = jnp.concatenate(plan.xor_order(up_pieces, plan.dp), axis=1).astype(F32)
    modulation_gradient = jnp.where(
        plan.top == 0, jnp.stack([sums[:6], other_sums[:6]]), jnp.stack([other_sums[:6], sums[:6]])
    )
    sums = sums + other_sums
    for bit in plan.dp_bits:
        sums = sums + plan.over_dp(sums, bit)
    small_grads = lax.dynamic_index_in_dim(
        sums.reshape(12, plan.total, shard_rows), plan.me, 1, keepdims=False
    )
    return (
        layer_output,
        latents_gradient,
        context_gradient.astype(F32),
        modulation_gradient,
        small_grads[:6],
        self_gradients[:, :width],
        self_gradients[:, width : 2 * width],
        self_gradients[:, 2 * width :],
        selfout_gradient,
        small_grads[6],
        small_grads[7],
        small_grads[8],
        small_grads[9],
        crossquery_gradient,
        crosskey_gradient,
        crossvalue_gradient,
        crossout_gradient,
        small_grads[10],
        small_grads[11],
        upmatrix_gradient,
        downmatrix_gradient,
    )


def solution(mesh):
    tokens = P("dp", "seq", None)
    clip = P("dp", None, None)
    table = P(None, ("dp", "seq"))
    matrix = P(("dp", "seq"), None)
    gain = P(("dp", "seq"))
    weights = (matrix,) * 4 + (gain,) * 4 + (matrix,) * 4 + (gain,) * 2 + (matrix,) * 2
    return jax.shard_map(
        functools.partial(body, Plan(mesh)),
        mesh=mesh,
        in_specs=(tokens, tokens, clip, tokens, table) + weights,
        out_specs=(tokens, tokens, tokens, clip, table) + weights,
        check_vma=False,
    )
```

```python
import functools
import math

import jax
import jax.numpy as jnp
import numpy as np
from jax import lax
from jax.experimental import pallas as pl
from jax.experimental.pallas import tpu as pltpu
from jax.sharding import PartitionSpec as P

HEADS = 12
HEAD_DIM = 128
GRID_H = 32
GRID_W = 32
EPS = 1e-06
BF = jnp.bfloat16
F32 = jnp.float32
SCALE = HEAD_DIM ** (-0.5)
SCALE_LOG2 = SCALE * math.log2(math.e)


def layer_norm(values):
    center = values - jnp.mean(values, axis=-1, keepdims=True)
    return center * lax.rsqrt(jnp.mean(center * center, axis=-1, keepdims=True) + EPS)


def layer_norm_back(values, gradient):
    center = values - jnp.mean(values, axis=-1, keepdims=True)
    inverse = lax.rsqrt(jnp.mean(center * center, axis=-1, keepdims=True) + EPS)
    normed = center * inverse
    return inverse * (
        gradient
        - jnp.mean(gradient, axis=-1, keepdims=True)
        - normed * jnp.mean(gradient * normed, axis=-1, keepdims=True)
    )


def gelu_tanh(values):
    return jax.nn.gelu(values, approximate=True)


def dot_nn(left, right, out=F32):
    return lax.dot_general(left, right, (((1,), (0,)), ((), ())), preferred_element_type=F32).astype(out)


def dot_nt(left, right, out=F32):
    return lax.dot_general(left, right, (((1,), (1,)), ((), ())), preferred_element_type=F32).astype(out)


def dot_tn(left, right, out=F32):
    return lax.dot_general(left, right, (((0,), (0,)), ((), ())), preferred_element_type=F32).astype(out)


def rotary_tables(positions):
    pairs = HEAD_DIM // 2
    side = pairs // 3
    lead = pairs - 2 * side

    def rates(number):
        return np.power(np.float32(10000.0), -np.arange(number, dtype=np.float32) / np.float32(number))

    def lanes(start, values):
        row = np.zeros((pairs,), np.float32)
        row[start : start + len(values)] = values
        return np.repeat(row, 2)[None]

    frame = (positions // (GRID_H * GRID_W)).astype(F32)[:, None]
    line = (positions // GRID_W % GRID_H).astype(F32)[:, None]
    column = (positions % GRID_W).astype(F32)[:, None]
    angles = (
        frame * lanes(0, rates(lead))
        + line * lanes(lead, rates(side))
        + column * lanes(lead + side, rates(side))
    )
    even = (np.arange(HEAD_DIM) % 2 == 0)[None]
    sine = jnp.sin(angles)
    return jnp.cos(angles), jnp.where(even, -sine, 0.0), jnp.where(even, 0.0, sine)


def turn(values, cosine, following, previous):
    return (
        values * cosine
        + pltpu.roll(values, HEAD_DIM - 1, 1) * following
        + pltpu.roll(values, 1, 1) * previous
    )


def head_lanes(head):
    return slice(head * HEAD_DIM, (head + 1) * HEAD_DIM)


def row_block(rows):
    return 128 if rows % 128 == 0 else rows


def row_spec(block, width):
    return pl.BlockSpec((block, width), lambda step: (step, 0))


def fixed_spec(width):
    return pl.BlockSpec((1, width), lambda step: (0, 0))


def params(mebibytes):
    return pltpu.CompilerParams(vmem_limit_bytes=mebibytes * 2**20)


def normed_turned(raw_ref, gain_ref, tables, write):
    raw = raw_ref[...]
    inverse = lax.rsqrt(jnp.mean(raw * raw, axis=-1, keepdims=True) + EPS)
    normed = raw * inverse * gain_ref[...]
    for head in range(HEADS):
        piece = normed[:, head_lanes(head)]
        if tables is not None:
            piece = turn(piece, *tables)
        write(head, piece.astype(BF))


def self_post(raw, gain_query, gain_key, tables, groups):
    rows, width = raw.shape[0], raw.shape[1] // 3
    block = row_block(rows)
    per_group = HEADS // groups

    def kernel(query_ref, key_ref, value_ref, gq_ref, gk_ref, cos_ref, next_ref, last_ref, query_out, *outs):
        turns = (cos_ref[...], next_ref[...], last_ref[...])

        def write_query(head, piece):
            query_out[:, head_lanes(head)] = piece

        def write_key(head, piece):
            start = (head % per_group) * 2 * HEAD_DIM
            outs[head // per_group][:, start : start + HEAD_DIM] = piece

        normed_turned(query_ref, gq_ref, turns, write_query)
        normed_turned(key_ref, gk_ref, turns, write_key)
        for head in range(HEADS):
            start = (head % per_group) * 2 * HEAD_DIM + HEAD_DIM
            outs[head // per_group][:, start : start + HEAD_DIM] = value_ref[:, head_lanes(head)].astype(BF)

    out_width = per_group * 2 * HEAD_DIM
    return pl.pallas_call(
        kernel,
        grid=(rows // block,),
        in_specs=[pl.BlockSpec((block, width), lambda step, part=part: (step, part)) for part in range(3)]
        + [fixed_spec(width)] * 2
        + [row_spec(block, HEAD_DIM)] * 3,
        out_specs=[row_spec(block, width)] + [row_spec(block, out_width)] * groups,
        out_shape=[jax.ShapeDtypeStruct((rows, width), BF)]
        + [jax.ShapeDtypeStruct((rows, out_width), BF)] * groups,
        compiler_params=params(32),
        cost_estimate=pl.CostEstimate(flops=rows * width * 20, bytes_accessed=rows * width * 18, transcendentals=0),
        name="self_post",
    )(raw, raw, raw, gain_query, gain_key, *tables)


def query_post(raw, gain):
    rows, width = raw.shape
    block = row_block(rows)

    def kernel(raw_ref, gain_ref, out_ref):
        def write(head, piece):
            out_ref[:, head_lanes(head)] = piece

        normed_turned(raw_ref, gain_ref, None, write)

    return pl.pallas_call(
        kernel,
        grid=(rows // block,),
        in_specs=[row_spec(block, width), fixed_spec(width)],
        out_specs=row_spec(block, width),
        out_shape=jax.ShapeDtypeStruct((rows, width), BF),
        compiler_params=params(24),
        cost_estimate=pl.CostEstimate(flops=rows * width * 10, bytes_accessed=rows * width * 6, transcendentals=0),
        name="query_post",
    )(raw, gain)


def text_post(raw, gain):
    rows, width = raw.shape[0], raw.shape[1] // 2
    block = row_block(rows)

    def kernel(key_ref, value_ref, gain_ref, out_ref):
        def write(head, piece):
            out_ref[:, 2 * head * HEAD_DIM : (2 * head + 1) * HEAD_DIM] = piece

        normed_turned(key_ref, gain_ref, None, write)
        for head in range(HEADS):
            start = (2 * head + 1) * HEAD_DIM
            out_ref[:, start : start + HEAD_DIM] = value_ref[:, head_lanes(head)].astype(BF)

    return pl.pallas_call(
        kernel,
        grid=(rows // block,),
        in_specs=[pl.BlockSpec((block, width), lambda step, part=part: (step, part)) for part in range(2)]
        + [fixed_spec(width)],
        out_specs=row_spec(block, 2 * width),
        out_shape=jax.ShapeDtypeStruct((rows, 2 * width), BF),
        compiler_params=params(24),
        cost_estimate=pl.CostEstimate(flops=rows * width * 10, bytes_accessed=rows * width * 12, transcendentals=0),
        name="text_post",
    )(raw, raw, gain)


def norm_back(raw, gain, gradient):
    inverse = lax.rsqrt(jnp.mean(raw * raw, axis=-1, keepdims=True) + EPS)
    normed = raw * inverse
    gained = gradient * gain
    back = (gained - normed * jnp.mean(gained * normed, axis=-1, keepdims=True)) * inverse
    return back, jnp.sum(gradient * normed, axis=0, keepdims=True)


def turned_back(piece, turns):
    return piece if turns is None else turn(piece, turns[0], -turns[1], -turns[2])


def accumulate(ref, term):
    @pl.when(pl.program_id(0) == 0)
    def _():
        ref[...] = jnp.zeros_like(ref)

    ref[...] += term


def self_query_back(gradients, raw, gain, tables):
    rows, width = raw.shape[0], raw.shape[1] // 3
    block = row_block(rows)
    groups = len(gradients)
    per_group = HEADS // groups

    def kernel(*refs):
        grads = refs[:groups]
        raw_ref, gain_ref, cos_ref, next_ref, last_ref, low_ref, gain_out = refs[groups:]
        turns = (cos_ref[...], next_ref[...], last_ref[...])
        pieces = [
            turned_back(grads[head // per_group][:, head_lanes(head % per_group)], turns)
            for head in range(HEADS)
        ]
        back, term = norm_back(raw_ref[...], gain_ref[...], jnp.concatenate(pieces, axis=1))
        low_ref[...] = back.astype(BF)
        accumulate(gain_out, term)

    return pl.pallas_call(
        kernel,
        grid=(rows // block,),
        in_specs=[row_spec(block, per_group * HEAD_DIM)] * groups
        + [row_spec(block, width), fixed_spec(width)]
        + [row_spec(block, HEAD_DIM)] * 3,
        out_specs=[row_spec(block, width), fixed_spec(width)],
        out_shape=[jax.ShapeDtypeStruct((rows, width), BF), jax.ShapeDtypeStruct((1, width), F32)],
        compiler_params=params(32),
        cost_estimate=pl.CostEstimate(flops=rows * width * 15, bytes_accessed=rows * width * 10, transcendentals=0),
        name="self_query_back",
    )(*gradients, raw, gain, *tables)


def self_keyvalue_back(gradients, raw, gain, tables):
    rows, width = raw.shape[0], raw.shape[1] // 3
    block = row_block(rows)
    groups = len(gradients)
    per_group = HEADS // groups

    def kernel(*refs):
        grads = refs[:groups]
        raw_ref, gain_ref, cos_ref, next_ref, last_ref, low_ref, gain_out = refs[groups:]
        turns = (cos_ref[...], next_ref[...], last_ref[...])
        pieces = []
        for head in range(HEADS):
            start = (head % per_group) * 2 * HEAD_DIM
            ref = grads[head // per_group]
            pieces.append(turned_back(ref[:, start : start + HEAD_DIM], turns))
            value = ref[:, start + HEAD_DIM : start + 2 * HEAD_DIM].astype(BF)
            low_ref[:, width + head * HEAD_DIM : width + (head + 1) * HEAD_DIM] = value
        back, term = norm_back(raw_ref[...], gain_ref[...], jnp.concatenate(pieces, axis=1))
        low_ref[:, :width] = back.astype(BF)
        accumulate(gain_out, term)

    return pl.pallas_call(
        kernel,
        grid=(rows // block,),
        in_specs=[row_spec(block, per_group * 2 * HEAD_DIM)] * groups
        + [pl.BlockSpec((block, width), lambda step: (step, 1)), fixed_spec(width)]
        + [row_spec(block, HEAD_DIM)] * 3,
        out_specs=[row_spec(block, 2 * width), fixed_spec(width)],
        out_shape=[jax.ShapeDtypeStruct((rows, 2 * width), BF), jax.ShapeDtypeStruct((1, width), F32)],
        compiler_params=params(32),
        cost_estimate=pl.CostEstimate(flops=rows * width * 15, bytes_accessed=rows * width * 18, transcendentals=0),
        name="self_keyvalue_back",
    )(*gradients, raw, gain, *tables)


def query_back(gradient, raw, gain):
    rows, width = raw.shape
    block = row_block(rows)

    def kernel(grad_ref, raw_ref, gain_ref, low_ref, gain_out):
        back, term = norm_back(raw_ref[...], gain_ref[...], grad_ref[...])
        low_ref[...] = back.astype(BF)
        accumulate(gain_out, term)

    return pl.pallas_call(
        kernel,
        grid=(rows // block,),
        in_specs=[row_spec(block, width), row_spec(block, width), fixed_spec(width)],
        out_specs=[row_spec(block, width), fixed_spec(width)],
        out_shape=[jax.ShapeDtypeStruct((rows, width), BF), jax.ShapeDtypeStruct((1, width), F32)],
        compiler_params=params(24),
        cost_estimate=pl.CostEstimate(flops=rows * width * 15, bytes_accessed=rows * width * 10, transcendentals=0),
        name="query_back",
    )(gradient, raw, gain)


def text_back(gradient, raw, gain):
    rows, width = raw.shape[0], raw.shape[1] // 2
    block = row_block(rows)

    def kernel(grad_ref, raw_ref, gain_ref, low_ref, gain_out):
        pieces = []
        for head in range(HEADS):
            start = 2 * head * HEAD_DIM
            pieces.append(grad_ref[:, start : start + HEAD_DIM])
            value = grad_ref[:, start + HEAD_DIM : start + 2 * HEAD_DIM].astype(BF)
            low_ref[:, width + head * HEAD_DIM : width + (head + 1) * HEAD_DIM] = value
        back, term = norm_back(raw_ref[...], gain_ref[...], jnp.concatenate(pieces, axis=1))
        low_ref[:, :width] = back.astype(BF)
        accumulate(gain_out, term)

    return pl.pallas_call(
        kernel,
        grid=(rows // block,),
        in_specs=[row_spec(block, 2 * width), row_spec(block, width), fixed_spec(width)],
        out_specs=[row_spec(block, 2 * width), fixed_spec(width)],
        out_shape=[jax.ShapeDtypeStruct((rows, 2 * width), BF), jax.ShapeDtypeStruct((1, width), F32)],
        compiler_params=params(24),
        cost_estimate=pl.CostEstimate(flops=rows * width * 15, bytes_accessed=rows * width * 16, transcendentals=0),
        name="text_back",
    )(gradient, raw, gain)


def attend(query, chunks, base, heads):
    rows = query.shape[0]
    count = len(chunks)
    keys = chunks[0].shape[0]

    def kernel(query_ref, *refs):
        out_ref, log_ref = refs[count:]
        query_head = query_ref[...]
        scores = [dot_nt(ref[:, :HEAD_DIM], query_head) for ref in refs[:count]]
        peak = functools.reduce(
            jnp.maximum, [jnp.max(score, axis=0, keepdims=True) for score in scores]
        )
        shift = peak * SCALE_LOG2
        total = jnp.zeros((1, rows), F32)
        summed = jnp.zeros((HEAD_DIM, rows), F32)
        for ref, score in zip(refs[:count], scores):
            weight = jnp.exp2(score * SCALE_LOG2 - shift)
            total += jnp.sum(weight, axis=0, keepdims=True)
            summed += dot_tn(ref[:, HEAD_DIM:], weight.astype(BF))
        out_ref[...] = (summed / total).T.astype(BF)
        log_ref[0] = shift + jnp.log2(total)

    return pl.pallas_call(
        kernel,
        grid=(heads,),
        in_specs=[pl.BlockSpec((rows, HEAD_DIM), lambda head: (0, base + head))]
        + [pl.BlockSpec((keys, 2 * HEAD_DIM), lambda head: (0, head))] * count,
        out_specs=[
            pl.BlockSpec((rows, HEAD_DIM), lambda head: (0, head)),
            pl.BlockSpec((1, 1, rows), lambda head: (head, 0, 0)),
        ],
        out_shape=[
            jax.ShapeDtypeStruct((rows, heads * HEAD_DIM), BF),
            jax.ShapeDtypeStruct((heads, 1, rows), F32),
        ],
        compiler_params=params(40),
        cost_estimate=pl.CostEstimate(
            flops=heads * rows * keys * count * HEAD_DIM * 4 * 2,
            bytes_accessed=heads * HEAD_DIM * 2 * (2 * rows + 2 * keys * count),
            transcendentals=heads * rows * keys * count,
        ),
        name="attend",
    )(query, *chunks)


def attend_back(query, chunks, gradient, logs, base, heads):
    rows = query.shape[0]
    count = len(chunks)
    keys = chunks[0].shape[0]

    def kernel(query_ref, grad_ref, log_ref, *refs):
        query_grad = refs[count]
        query_head, grad_head = query_ref[...], grad_ref[...]
        shift = log_ref[0]
        weights, value_grads = [], []
        delta = jnp.zeros((1, rows), F32)
        for ref in refs[:count]:
            weight = jnp.exp2(dot_nt(ref[:, :HEAD_DIM], query_head) * SCALE_LOG2 - shift)
            value_grad = dot_nt(ref[:, HEAD_DIM:], grad_head)
            delta += jnp.sum(weight * value_grad, axis=0, keepdims=True)
            weights.append(weight)
            value_grads.append(value_grad)
        summed = jnp.zeros((HEAD_DIM, rows), F32)
        out = refs[count + 1]
        for at, (ref, weight, value_grad) in enumerate(zip(refs[:count], weights, value_grads)):
            score_grad = (weight * (value_grad - delta)).astype(BF)
            out[at, :, :HEAD_DIM] = (dot_nn(score_grad, query_head) * SCALE).astype(BF)
            out[at, :, HEAD_DIM:] = dot_nn(weight.astype(BF), grad_head).astype(BF)
            summed += dot_tn(ref[:, :HEAD_DIM], score_grad)
        query_grad[...] = (summed * SCALE).T

    return pl.pallas_call(
        kernel,
        grid=(heads,),
        in_specs=[
            pl.BlockSpec((rows, HEAD_DIM), lambda head: (0, base + head)),
            pl.BlockSpec((rows, HEAD_DIM), lambda head: (0, base + head)),
            pl.BlockSpec((1, 1, rows), lambda head: (head, 0, 0)),
        ]
        + [pl.BlockSpec((keys, 2 * HEAD_DIM), lambda head: (0, head))] * count,
        out_specs=[
            pl.BlockSpec((rows, HEAD_DIM), lambda head: (0, head)),
            pl.BlockSpec((count, keys, 2 * HEAD_DIM), lambda head: (0, 0, head)),
        ],
        out_shape=[
            jax.ShapeDtypeStruct((rows, heads * HEAD_DIM), F32),
            jax.ShapeDtypeStruct((count, keys, heads * 2 * HEAD_DIM), BF),
        ],
        compiler_params=params(40),
        cost_estimate=pl.CostEstimate(
            flops=heads * rows * keys * count * HEAD_DIM * 10 * 2,
            bytes_accessed=heads * HEAD_DIM * 2 * (5 * rows + 4 * keys * count),
            transcendentals=heads * rows * keys * count,
        ),
        name="attend_back",
    )(query, gradient, logs, *chunks)


def place_rows(numbers, left, right, rows, total):
    slots, _, right_width = right[0][0].shape
    left_width = left[0][0].shape[2]
    count = len(left)
    extra = left_width > right_width

    def kernel(numbers_ref, *refs):
        whole_ref = refs[4 * count]
        step = pl.program_id(0)
        for at in range(count):
            for core in range(2):

                @pl.when((step // slots == at) & (numbers_ref[0] == core))
                def _():
                    for other in range(2):
                        place = pl.ds((other ^ core) * rows, rows)
                        left_ref, right_ref = refs[4 * at + other], refs[4 * at + 2 + other]
                        whole_ref[place, :right_width] = left_ref[0, :, :right_width]
                        whole_ref[place, right_width:] = right_ref[0]
                        if extra:
                            refs[4 * count + 1][place] = left_ref[0, :, right_width:]

    def source(at, width):
        return pl.BlockSpec(
            (1, rows, width),
            lambda step, numbers_ref: (jnp.clip(step - at * slots, 0, slots - 1), 0, 0),
        )

    def index(step, numbers_ref):
        return (numbers_ref[step + 1], 0)

    in_specs, arrays = [], []
    for at in range(count):
        in_specs += [source(at, left_width)] * 2 + [source(at, right_width)] * 2
        arrays += [*left[at], *right[at]]
    return pl.pallas_call(
        kernel,
        grid_spec=pltpu.PrefetchScalarGridSpec(
            num_scalar_prefetch=1,
            grid=(count * slots,),
            in_specs=in_specs,
            out_specs=[
                pl.BlockSpec((2 * rows, 2 * right_width), index),
                pl.BlockSpec((2 * rows, left_width - right_width), index),
            ][: 1 + extra],
        ),
        out_shape=[
            jax.ShapeDtypeStruct((total, 2 * right_width), BF),
            jax.ShapeDtypeStruct((total, left_width - right_width), BF),
        ][: 1 + extra],
        compiler_params=params(32),
        cost_estimate=pl.CostEstimate(flops=0, bytes_accessed=8 * total * right_width, transcendentals=0),
        name="place_rows",
    )(numbers, *arrays)


def after(value, *others):
    return lax.optimization_barrier((value,) + others)[0]


def together(*values):
    return lax.optimization_barrier(values)


class Plan:
    def __init__(self, mesh):
        self.dp_n = mesh.shape["dp"]
        self.seq_n = mesh.shape["seq"]
        self.total = self.dp_n * self.seq_n
        self.half = self.seq_n // 2
        self.columns = self.seq_n // 2
        self.groups = 3 if self.half <= 4 else 1
        self.dp_bits = [1 << i for i in range(self.dp_n.bit_length() - 1)]
        self.group_bits = [1 << i for i in range(self.half.bit_length() - 1)]

    def start(self):
        self.dp = lax.axis_index("dp")
        self.seq = lax.axis_index("seq")
        self.me = self.dp * self.seq_n + self.seq
        self.core = self.seq % 2
        self.column = self.seq // 2
        self.top = self.seq // self.half

    def over_seq(self, value, offset):
        return lax.ppermute(value, "seq", [(i, i ^ offset) for i in range(self.seq_n)])

    def over_dp(self, value, offset):
        return lax.ppermute(value, "dp", [(i, i ^ offset) for i in range(self.dp_n)])


    def shift(self, value):
        own = lax.dynamic_index_in_dim(value, self.top, 0, keepdims=False)
        other = lax.dynamic_index_in_dim(value, 1 - self.top, 0, keepdims=False)
        return jnp.concatenate([own, self.over_seq(other, self.half)], axis=0)

    def unshift(self, value):
        rows = value.shape[0] // 2
        own, other = value[:rows], self.over_seq(value[rows:], self.half)
        return jnp.where(self.top == 0, jnp.stack([own, other]), jnp.stack([other, own]))


    def group_gather(self, value, *behind):
        held = {0: after(value, *behind) if behind else value}
        for bit in reversed(self.group_bits):
            held.update({at ^ bit: self.over_seq(one, bit) for at, one in list(held.items())})
        return held

    def chunks(self, held):
        order = [0]
        for bit in reversed(self.group_bits):
            order = order + [at ^ bit for at in order]
        return [held[at] for at in order]

    def group_scatter(self, parts):
        for bit in self.group_bits:
            half = parts.shape[0] // 2
            sent = self.over_seq(parts[half:].astype(BF), bit)
            parts = parts[:half].astype(F32) + sent.astype(F32)
        return parts[0]


    def gather_columns(self, shard):
        return jnp.stack([shard] + [self.over_seq(shard, 2 * k) for k in range(1, self.columns)])

    def gather_dp(self, sides, orders, number):
        return [
            {at ^ order[number]: self.over_dp(one, order[number]) for at, one in side.items()}
            for side, order in zip(sides, orders)
        ]

    def gather_place(self, sides):
        left, right = [{at: (one, self.over_seq(one, 1)) for at, one in side.items()} for side in sides]
        slots = self.columns
        rows, width = right[0][0].shape[1:]
        if rows % 16 == 0:
            blocks = [(self.dp ^ at) * slots + (self.column ^ slot) for at in left for slot in range(slots)]
            numbers = jnp.stack([self.core] + blocks).astype(jnp.int32)
            return place_rows(
                numbers, list(left.values()), [right[at] for at in left], rows, self.total * rows
            )
        wholes = []
        for held in (left, right):
            pieces = [
                held[number // self.seq_n][number % 2][(number % self.seq_n) // 2]
                for number in range(self.total)
            ]
            stacked = jnp.stack(pieces)

            def place(number, out):
                return lax.dynamic_update_index_in_dim(
                    out, self.pick(stacked, number, 0), number ^ self.me, 0
                )

            ordered = lax.fori_loop(0, self.total, place, jnp.zeros_like(stacked))
            wholes.append(ordered.reshape(self.total * rows, -1))
        left, right = wholes
        return [jnp.concatenate([left[:, :width], right], axis=1), left[:, width:]]

    def xor_order(self, pieces, number):
        bit = 1
        while bit < len(pieces):
            swapped = (number // bit) % 2 == 1
            pieces = [jnp.where(swapped, pieces[i ^ bit], pieces[i]) for i in range(len(pieces))]
            bit *= 2
        return pieces

    def pick(self, value, number, axis):
        return lax.dynamic_index_in_dim(value, number, axis, keepdims=False)

    def scatter_columns(self, value, axis, wire):
        total = self.pick(value, self.column, axis).astype(F32)
        for k in range(1, self.columns):
            sent = self.over_seq(self.pick(value, self.column ^ k, axis).astype(wire), 2 * k)
            total = total + sent.astype(F32)
        return total


    def scatter_core(self, *values):
        bits = len(self.dp_bits)
        values = [
            one.reshape((2,) * bits + (self.columns, 2, one.shape[0] // self.total, one.shape[1]))
            for one in values
        ]
        kept, sent = [
            jnp.concatenate([self.pick(one, core, bits + 1) for one in values], axis=-1)
            for core in (self.core, 1 - self.core)
        ]
        return kept, self.over_seq(sent, 1)

    def scatter_dp(self, halves, done, bit):
        value = (halves[0].astype(F32) + halves[1].astype(F32)).astype(BF)
        axis = [one for one in reversed(self.dp_bits) if one not in done].index(bit)
        mine = (self.dp // bit) % 2
        sent = self.over_dp(self.pick(value, 1 - mine, axis), bit)
        return self.pick(value, mine, axis), sent

    def scatter_pair(self, pair, orders, number):
        return [
            self.scatter_dp(halves, order[:number], order[number]) for halves, order in zip(pair, orders)
        ]

    def scatter_pair_last(self, pair):
        value = jnp.concatenate([halves[0].astype(F32) + halves[1].astype(F32) for halves in pair], axis=-1)
        width = pair[0][0].shape[-1]
        total = self.scatter_columns(value.astype(BF), 0, BF)
        return total[:, :width], total[:, width:]


def body(
    plan,
    latents,
    context,
    modulation,
    cotangent,
    modtable,
    selfquery,
    selfkey,
    selfvalue,
    selfout,
    querygain,
    keygain,
    normgain,
    normbias,
    crossquery,
    crosskey,
    crossvalue,
    crossout,
    crossqgain,
    crosskgain,
    upmatrix,
    downmatrix,
):
    plan.start()
    width = latents.shape[2]
    dp_n, seq_n, columns = plan.dp_n, plan.seq_n, plan.columns
    everywhere = ("dp", "seq")
    rows_one = latents.shape[1]
    shard_rows = selfquery.shape[0]
    hidden = upmatrix.shape[1]
    part = hidden // dp_n
    xy, yx = plan.dp_bits, list(reversed(plan.dp_bits))

    small = jnp.concatenate(
        [modtable.T]
        + [gain[:, None] for gain in (querygain, keygain, normgain, normbias, crossqgain, crosskgain)]
        + [jnp.zeros((shard_rows, HEAD_DIM - 12), BF)],
        axis=1,
    )
    middle = 3 * width // 2
    side = jnp.concatenate([selfquery, selfkey, selfvalue], axis=1)
    both = plan.gather_columns(jnp.concatenate([side[:, :middle], small, side[:, middle:]], axis=1))
    token_rows = plan.shift(latents)
    up_parts = [
        lax.dynamic_slice_in_dim(upmatrix, (plan.dp ^ j) * part, part, 1) for j in range(dp_n)
    ]
    up_parts = [plan.over_dp(one, j) if j else one for j, one in enumerate(up_parts)]
    both, token_rows, up_parts = together(both, token_rows, up_parts)
    up_shard = jnp.concatenate(plan.xor_order(up_parts, plan.dp), axis=0)
    edge = middle + HEAD_DIM
    first = [{0: both[:, :, :edge]}, {0: both[:, :, edge:]}]

    others = after(jnp.concatenate([selfout, crossquery, crossout, crosskey, crossvalue], axis=1), both)
    others = plan.gather_columns(others)
    for number in range(len(xy)):
        arrived = plan.gather_dp(first, (xy, yx), number)
        if number + 1 < len(xy):
            arrived = together(*arrived)
        else:
            *arrived, others = together(*arrived, others)
        first = [{**side, **more} for side, more in zip(first, arrived)]
    whole_self, small_all = plan.gather_place(first)
    small_placed = small_all
    small_all = small_all.T[:12].astype(F32)
    edge = 5 * width // 2
    second = [{0: others[:, :, :edge]}, {0: others[:, :, edge:]}]

    mod_rows = lax.dynamic_index_in_dim(modulation, plan.top, 0, keepdims=False) + small_all[:6]
    shift_a, scale_a, gate_a, shift_m, scale_m, gate_m = [mod_rows[i : i + 1] for i in range(6)]
    gain_query, gain_key, gain_norm, bias_norm, gain_crossq, gain_crossk = [
        small_all[i : i + 1] for i in range(6, 12)
    ]
    span = jnp.arange(rows_one, dtype=jnp.int32)
    positions = jnp.concatenate(
        [plan.seq * rows_one + span, (plan.seq ^ plan.half) * rows_one + span]
    )
    tables = rotary_tables(positions)

    latent_rows = token_rows.astype(F32)
    normed_a = layer_norm(latent_rows)
    attn_in = (normed_a * (1.0 + scale_a) + shift_a).astype(BF)
    self_raw = dot_nn(attn_in, whole_self)
    shifted = plan.shift(after(jnp.concatenate([cotangent, context], axis=1), small_placed))
    *arrived, self_raw = together(*plan.gather_dp(second, (xy, yx), 0), self_raw)
    second = [{**side, **more} for side, more in zip(second, arrived)]
    queries, *keyvalues = self_post(self_raw, gain_query, gain_key, tables, plan.groups)
    keyvalues, shifted = together(keyvalues, shifted)
    text_one = context.shape[1]
    step = rows_one + text_one
    grad_rows = jnp.concatenate([shifted[:rows_one], shifted[step : step + rows_one]])
    text_rows = jnp.concatenate([shifted[rows_one:step], shifted[step + rows_one :]])
    per_group = HEADS // plan.groups
    gathered = []
    for group, one in enumerate(keyvalues):
        behind = [gathered[-1][plan.group_bits[-1]]] if gathered else []
        gathered.append(plan.group_gather(one, *behind))
        if group < 2:
            number = len(xy) - 1
            if group == 0:
                for early in range(1, number):
                    arrived = plan.gather_dp(second, (xy, yx), early)
                    second = [{**side, **more} for side, more in zip(second, arrived)]
                half = len(second[0]) // 2
                parts = [dict(list(side.items())[:half]) for side in second]
                whole_second = [dict(side) for side in second]
            else:
                parts = [dict(list(side.items())[half:]) for side in second]
                parts, arrived = together(parts, arrived)
            if plan.groups == 1:
                parts = second
            bit = plan.group_bits[-1]
            arrived, gathered[-1][bit] = together(
                plan.gather_dp(parts, (xy, yx), number), gathered[-1][bit]
            )
            whole_second = [{**side, **more} for side, more in zip(whole_second, arrived)]
    second = whole_second
    arrived = gathered[-1][plan.group_bits[-1]]
    (whole_others,) = plan.gather_place(second)[:1]
    whole_selfout, whole_crossquery, whole_crossout = [
        whole_others[:, i * width : (i + 1) * width] for i in range(3)
    ]
    whole_crosstext = whole_others[:, 3 * width :]
    text_raw = dot_nn(text_rows, whole_crosstext)
    text_keyvalues = text_post(text_raw, gain_crossk)
    gathered[-1], text_keyvalues = together(gathered[-1], text_keyvalues)
    cross_gathered = plan.group_gather(text_keyvalues)
    up_shard = after(up_shard, arrived)
    whole_up = lax.all_gather(up_shard, "seq", axis=0, tiled=True)
    whole_up = (
        whole_up.reshape(seq_n, dp_n, shard_rows, part)
        .transpose(1, 0, 2, 3)
        .reshape(plan.total * shard_rows, part)
    )
    self_outs, self_logs = [], []
    for group in range(plan.groups):
        out, logs = attend(queries, plan.chunks(gathered[group]), group * per_group, per_group)
        self_outs.append(out)
        self_logs.append(logs)
    down_shard = after(downmatrix, cross_gathered[plan.group_bits[-1]])
    whole_down = lax.all_gather(down_shard, "seq", axis=0, tiled=True)
    out_grad = grad_rows.astype(F32)
    down_grad = (out_grad * gate_m).astype(BF)
    down_grads = [down_grad] + [plan.over_dp(down_grad, j) for j in range(1, dp_n)]
    attended = jnp.concatenate(self_outs, axis=1)
    self_branch = dot_nn(attended, whole_selfout)
    hidden_one = latent_rows + self_branch * gate_a

    cross_in = (layer_norm(hidden_one) * gain_norm + bias_norm).astype(BF)
    crossq_raw = dot_nn(cross_in, whole_crossquery)
    cross_queries = query_post(crossq_raw, gain_crossq)
    crossed, cross_logs = attend(cross_queries, plan.chunks(cross_gathered), 0, HEADS)
    crossed, down_grads = together(crossed, down_grads)
    hidden_two = hidden_one + dot_nn(crossed, whole_crossout)

    normed_m = layer_norm(hidden_two)
    mlp_in = (normed_m * (1.0 + scale_m) + shift_m).astype(BF)
    received = [plan.over_dp(mlp_in, j) for j in range(1, dp_n)]
    mlp_ins, activations, up_grads, mlp_grads = [mlp_in], [], [], []
    for j in range(dp_n):
        up_values = dot_nn(mlp_ins[j], whole_up)
        activation, gelu_back = jax.vjp(gelu_tanh, up_values)
        activations.append(activation.astype(BF))
        up_grads.append(gelu_back(dot_nt(down_grads[j], whole_down))[0].astype(BF))
        mlp_grads.append(dot_nt(up_grads[j], whole_up, BF if j else F32))
        if j + 1 < dp_n:
            one, activations[j] = together(received[j], activations[j])
            mlp_ins.append(one)
    mlp_sent = [plan.over_dp(mlp_grads[j], j) for j in range(1, dp_n)]

    up_in, down_in, _ = together(jnp.concatenate(mlp_ins), jnp.concatenate(activations), mlp_grads[0])
    down_term = dot_tn(down_in, jnp.concatenate(down_grads), BF)
    up_term = dot_tn(up_in, jnp.concatenate(up_grads), BF)
    up_term = (
        up_term.reshape(dp_n, seq_n, shard_rows, part)
        .transpose(1, 0, 2, 3)
        .reshape(plan.total * shard_rows, part)
    )
    mlp_sent, up_term = together(mlp_sent, up_term)
    downmatrix_gradient = lax.psum_scatter(down_term, "seq", scatter_dimension=0, tiled=True).astype(F32)
    up_term = lax.psum_scatter(up_term, "seq", scatter_dimension=0, tiled=True)
    up_term = up_term.reshape(dp_n, shard_rows, part)
    mlp_grad = mlp_grads[0] + sum(one.astype(F32) for one in mlp_sent)
    activations, mlp_grad = together(activations, mlp_grad)
    down_all = [dot_nn(activations[j], whole_down, BF if j else F32) for j in range(dp_n)]
    down_sent = [plan.over_dp(down_all[j], j) for j in range(1, dp_n)]
    mlp_grad, down_all = together(mlp_grad, down_all)

    shift_m_grad = jnp.sum(mlp_grad, axis=0)
    scale_m_grad = jnp.sum(mlp_grad * normed_m, axis=0)
    two_grad = out_grad + layer_norm_back(hidden_two, mlp_grad * (1.0 + scale_m))
    cross_grad = two_grad.astype(BF)
    crossed_grad = dot_nt(cross_grad, whole_crossout, BF)
    crossout_term = dot_tn(crossed, cross_grad, BF)
    crossq_grad, cross_parts = attend_back(
        cross_queries, plan.chunks(cross_gathered), crossed_grad, cross_logs, 0, HEADS
    )
    cross_own = plan.group_scatter(cross_parts)
    crossq_low, crossq_gaingrad = query_back(crossq_grad, crossq_raw, gain_crossq)
    cross_sums = [plan.scatter_core(crossout_term), plan.scatter_core(dot_tn(cross_in, crossq_low, BF))]
    crossin_grad = dot_nt(crossq_low, whole_crossquery)
    normgain_grad = jnp.sum(crossin_grad * layer_norm(hidden_one), axis=0)
    normbias_grad = jnp.sum(crossin_grad, axis=0)
    one_grad = two_grad + layer_norm_back(hidden_one, crossin_grad * gain_norm)
    gate_a_grad = jnp.sum(one_grad * self_branch, axis=0)
    branch_grad = (one_grad * gate_a).astype(BF)
    branch_grad, cross_sums = together(branch_grad, cross_sums)
    cross_sums = plan.scatter_pair(cross_sums, (xy, yx), 0)
    attended_grad = dot_nt(branch_grad, whole_selfout, BF)
    query_grads, keyvalue_grads = [], []
    for group in range(plan.groups):
        if group:
            if group < len(xy):
                cross_sums = plan.scatter_pair(cross_sums, (xy, yx), group)
            attended_grad, cross_sums = together(attended_grad, cross_sums)
        query_grad, parts = attend_back(
            queries,
            plan.chunks(gathered[group]),
            attended_grad,
            self_logs[group],
            group * per_group,
            per_group,
        )
        if group == 0:
            query_grad, cross_own = together(query_grad, cross_own)
            text_low, crossk_gaingrad = text_back(cross_own, text_raw, gain_crossk)
            text_term = dot_tn(text_rows, text_low, BF)
            selfout_term = dot_tn(attended, branch_grad, BF)
            pieces = [
                (text_term[:, :width], selfout_term[:, : width // 2]),
                (text_term[:, width:], selfout_term[:, width // 2 :]),
            ]
            text_sums = [plan.scatter_core(*pair) for pair in pieces]
            context_gradient = plan.unshift(dot_nt(text_low, whole_crosstext, BF))
        if group == min(1, plan.groups - 1):
            query_grad, text_sums, context_gradient = together(query_grad, text_sums, context_gradient)
            text_sums = plan.scatter_pair(text_sums, (xy, yx), 0)
        if group == plan.groups - 1:
            for number in range(plan.groups, len(xy)):
                cross_sums = plan.scatter_pair(cross_sums, (xy, yx), number)
            query_grad, cross_sums, up_term = together(query_grad, cross_sums, up_term)
            crossout_gradient, crossquery_gradient = plan.scatter_pair_last(cross_sums)
            up_pieces = [plan.pick(up_term, plan.dp ^ j, 0) for j in range(dp_n)]
            up_pieces = [plan.over_dp(one, j) if j else one for j, one in enumerate(up_pieces)]
        query_grads.append(query_grad)
        keyvalue_grads.append(plan.group_scatter(parts))

    query_low, query_gaingrad = self_query_back(query_grads, self_raw, gain_query, tables)
    query_term = dot_tn(attn_in, query_low, BF)
    attn_grad = dot_nt(query_low, whole_self[:, :width])
    keyvalue_grads, attn_grad, query_term, text_sums, down_sent, up_pieces = together(
        keyvalue_grads, attn_grad, query_term, text_sums, down_sent, up_pieces
    )
    down_values = down_all[0] + sum(one.astype(F32) for one in down_sent)
    layer_low = (hidden_two + down_values * gate_m).astype(BF)
    gate_m_grad = jnp.sum(out_grad * down_values, axis=0)
    for number in range(1, len(xy)):
        text_sums = plan.scatter_pair(text_sums, (xy, yx), number)

    keyvalue_low, key_gaingrad = self_keyvalue_back(keyvalue_grads, self_raw, gain_key, tables)
    key_middle = middle - width
    left_term = dot_tn(attn_in, keyvalue_low[:, :key_middle], BF)
    right_term = dot_tn(attn_in, keyvalue_low[:, key_middle:], BF)
    self_sums = [
        plan.scatter_core(query_term, left_term),
        plan.scatter_core(right_term),
    ]
    kept_low, _ = together(keyvalue_low, (left_term, right_term))
    attn_grad = attn_grad + dot_nt(kept_low, whole_self[:, width:])
    attn_grad, self_sums, layer_low, crossout_gradient = together(
        attn_grad, self_sums, layer_low, crossout_gradient
    )
    layer_output = plan.unshift(layer_low)
    self_sums = plan.scatter_pair(self_sums, (xy, yx), 0)
    shift_a_grad = jnp.sum(attn_grad, axis=0)
    scale_a_grad = jnp.sum(attn_grad * normed_a, axis=0)
    latents_low = (one_grad + layer_norm_back(latent_rows, attn_grad * (1.0 + scale_a))).astype(BF)
    local_mod = jnp.stack(
        [shift_a_grad, scale_a_grad, gate_a_grad, shift_m_grad, scale_m_grad, gate_m_grad]
    )
    sums = jnp.concatenate(
        [
            local_mod,
            query_gaingrad,
            key_gaingrad,
            normgain_grad[None],
            normbias_grad[None],
            crossq_gaingrad,
            crossk_gaingrad,
        ]
    )
    for bit in plan.group_bits:
        sums = sums + plan.over_seq(sums, bit)
    other_sums = plan.over_seq(sums, plan.half)
    latents_low, other_sums, layer_output, text_sums = together(
        latents_low, other_sums, layer_output, text_sums
    )
    latents_gradient = plan.unshift(latents_low)
    for number in range(1, len(xy)):
        self_sums = plan.scatter_pair(self_sums, (xy, yx), number)
    self_sums, latents_gradient = together(self_sums, latents_gradient)
    latents_gradient = latents_gradient.astype(F32)
    left, right = plan.scatter_pair_last(
        [
            tuple(jnp.concatenate(side, axis=-1) for side in zip(*two))
            for two in zip(self_sums, text_sums)
        ]
    )
    self_gradients = jnp.concatenate([left[:, :middle], right[:, :middle]], axis=1)
    left, right = left[:, middle:], right[:, middle:]
    crosskey_gradient, crossvalue_gradient = left[:, :width], right[:, :width]
    selfout_gradient = jnp.concatenate([left[:, width:], right[:, width:]], axis=1)
    upmatrix_gradient = jnp.concatenate(plan.xor_order(up_pieces, plan.dp), axis=1).astype(F32)
    modulation_gradient = jnp.where(
        plan.top == 0, jnp.stack([sums[:6], other_sums[:6]]), jnp.stack([other_sums[:6], sums[:6]])
    )
    sums = sums + other_sums
    for bit in plan.dp_bits:
        sums = sums + plan.over_dp(sums, bit)
    small_grads = lax.dynamic_index_in_dim(
        sums.reshape(12, plan.total, shard_rows), plan.me, 1, keepdims=False
    )
    return (
        layer_output,
        latents_gradient,
        context_gradient.astype(F32),
        modulation_gradient,
        small_grads[:6],
        self_gradients[:, :width],
        self_gradients[:, width : 2 * width],
        self_gradients[:, 2 * width :],
        selfout_gradient,
        small_grads[6],
        small_grads[7],
        small_grads[8],
        small_grads[9],
        crossquery_gradient,
        crosskey_gradient,
        crossvalue_gradient,
        crossout_gradient,
        small_grads[10],
        small_grads[11],
        upmatrix_gradient,
        downmatrix_gradient,
    )


def solution(mesh):
    tokens = P("dp", "seq", None)
    clip = P("dp", None, None)
    table = P(None, ("dp", "seq"))
    matrix = P(("dp", "seq"), None)
    gain = P(("dp", "seq"))
    weights = (matrix,) * 4 + (gain,) * 4 + (matrix,) * 4 + (gain,) * 2 + (matrix,) * 2
    return jax.shard_map(
        functools.partial(body, Plan(mesh)),
        mesh=mesh,
        in_specs=(tokens, tokens, clip, tokens, table) + weights,
        out_specs=(tokens, tokens, tokens, clip, table) + weights,
        check_vma=False,
    )
```
